32 devices in a mesh: dp: 2 (over x), ctx: 8 (over z, core), tp: 2 (over y).
Axes of the slice: x: 2, y: 2, z: 4, core: 2. Of those that a mesh axis runs over, the one named last changes fastest.
Arguments:
- query: bfloat16 [2048, 12288], P(('dp', 'ctx'), 'tp'), parts along dimension 0
- keys: bfloat16 [2048, 1024], P(('dp', 'ctx'), 'tp'), parts along dimension 0
- values: bfloat16 [2048, 1024], P(('dp', 'ctx'), 'tp'), parts along dimension 0, may hold values from -6 to 6
- doc_lengths: int32 [32], P('dp'), parts along dimension 0, may hold values from 1 to 640, 1024 in all
- gain: bfloat16 [12288], P('tp'), may hold values from 0.5 to 1.5
Outputs:
- normed: bfloat16 [2048, 12288], P(('dp', 'ctx'), 'tp'), parts along dimension 0
The draws below stay inside these ranges and needn't reach their ends.
There are 2 independent parts, one for each index of `dp`. The reference program is written for one: setup_inputs(seed, part) draws one part's arguments, and reference() takes and returns one part's arrays. A program takes and returns all parts, laid end to end along the dimension named above; an argument that names none is the same for every part. Nothing has to cross between parts.
Inputs may be any that keep to these rules, and one draw needn't show every extreme that they name: `doc_lengths`: the lengths sum to 1024; the longest is exactly 640.
All inputs are finite; a program needn't handle non-finite values.
Results may differ from the reference program's by a relative error of at most 0.015.
Values may be sent and summed in bfloat16 or wider, within the bound.
A program may use at most 64 MiB of HBM per device.

```python
import math
import jax
import jax.numpy as jnp
import numpy as np
from jax import lax

QUERY_HEADS = 96
KEY_VALUE_HEADS = 8
HEAD_SIZE = 128
NDOC = 16
PACKED_TOKENS = 1024
LMAX = 640


def paired_rows(key):
    key_query, random_key_pair = jax.random.split(key)
    queries = jnp.clip(jax.random.normal(key_query, (PACKED_TOKENS, QUERY_HEADS * HEAD_SIZE), jnp.float32), -6.0, 6.0)
    key_row_block = jnp.clip(jax.random.normal(random_key_pair, (PACKED_TOKENS, KEY_VALUE_HEADS * HEAD_SIZE), jnp.float32), -6.0, 6.0)
    return (queries, key_row_block)


def draw_query(key, part):
    return paired_rows(key)[0].astype(jnp.bfloat16)


def draw_keys(key, part):
    return paired_rows(key)[1].astype(jnp.bfloat16)


def levels(stream_key, dims, cuts, smallest, high):
    factor_of, own = 1.0, jax.random.fold_in(stream_key, 6)
    for axis_at, parts in cuts:
        draws = jnp.exp(jax.random.uniform(jax.random.fold_in(own, axis_at), (parts,), jnp.float32, smallest / len(cuts), high / len(cuts)))
        factor_of = factor_of * jnp.repeat(draws, dims[axis_at] // parts).reshape([-1 if axis == axis_at else 1 for axis in range(len(dims))])
    return factor_of


def length_profile(count, total, bound, slope):
    weights = [(1 << 20) // math.isqrt(grade ** slope) + 1 for grade in range(2, count + 1)]
    spare, given = total - bound - (count - 1), [1] * (count - 1)
    while spare > 0:
        candidates = [i for i in range(count - 1) if given[i] < bound]
        whole, remaining = sum([weights[i] for i in candidates]), spare
        for i in candidates:
            more = min(bound - given[i], max(1, remaining * weights[i] // whole), spare)
            given[i] = given[i] + more
            spare = spare - more
    return np.array([bound] + given)


def ragged_sizes(rng, amount, total, limit, skew):
    if amount == 2:
        one = jax.random.randint(rng, (), max(1, total - limit), min(limit, total - 1) + 1)
        return jnp.stack([one, total - one])
    lengths = jnp.asarray(length_profile(amount, total, limit, skew), jnp.int32)
    twos = (amount - 1) // 2
    donor, receiver = lengths[1:1 + 2 * twos:2], lengths[2:2 + 2 * twos:2]
    room = jnp.minimum(donor - 1, limit - receiver)
    passed = jax.random.randint(jax.random.fold_in(rng, 1), (twos,), 0, 1 << 20) % (room + 1)
    lengths = lengths.at[1:1 + 2 * twos:2].set(donor - passed).at[2:2 + 2 * twos:2].set(receiver + passed)
    return lengths[jax.random.permutation(jax.random.fold_in(rng, 2), amount)]


def gaussian(stream_key, shape, width, reach, cuts=(), held_as=jnp.bfloat16):
    drawn = width * jax.random.normal(stream_key, shape, jnp.float32)
    if cuts:
        drawn = drawn * levels(stream_key, shape, cuts, -0.22, 0.18)
    return jnp.clip(drawn, -reach, reach).astype(held_as)


def setup_inputs(seed: int = 0, part: int = 0) -> dict:
    key_of = jax.random.split(jax.random.key(seed), 6)
    part_splits = jax.random.split(jax.random.fold_in(key_of[5], part), 6)
    query = draw_query(jax.random.fold_in(jax.random.fold_in(key_of[5], part), 71), part)
    keys = draw_keys(jax.random.fold_in(jax.random.fold_in(key_of[5], part), 71), part)
    values = gaussian(part_splits[2], (PACKED_TOKENS, KEY_VALUE_HEADS * HEAD_SIZE), 1.0, 6.0, ((0, 8), (1, 2)))
    doc_lengths = ragged_sizes(part_splits[3], NDOC, PACKED_TOKENS, LMAX, 2).astype(jnp.int32)
    gain = jnp.clip(1.0 + 0.1 * jax.random.normal(key_of[4], (QUERY_HEADS * HEAD_SIZE,), jnp.float32), 0.5, 1.5).astype(jnp.bfloat16)
    return dict(query=query, keys=keys, values=values, doc_lengths=doc_lengths, gain=gain)


def reference(query, keys, values, doc_lengths, gain):
    ends = jnp.cumsum(doc_lengths).astype(jnp.int32)
    positions = jnp.arange(PACKED_TOKENS, dtype=jnp.int32)
    doc_of = lax.optimization_barrier(jnp.sum((positions[:, None] >= ends[None, :]).astype(jnp.int32), axis=1))
    allowed = (doc_of[:, None] == doc_of[None, :]) & (positions[None, :] <= positions[:, None])
    query_group_ratio = QUERY_HEADS // KEY_VALUE_HEADS
    scale = HEAD_SIZE ** (-0.5)

    def one_head(head):
        group = head // query_group_ratio
        q_rows = lax.dynamic_slice(query, (jnp.int32(0), (head * HEAD_SIZE).astype(jnp.int32)), (PACKED_TOKENS, HEAD_SIZE))
        k_rows = lax.dynamic_slice(keys, (jnp.int32(0), (group * HEAD_SIZE).astype(jnp.int32)), (PACKED_TOKENS, HEAD_SIZE))
        v_rows = lax.dynamic_slice(values, (jnp.int32(0), (group * HEAD_SIZE).astype(jnp.int32)), (PACKED_TOKENS, HEAD_SIZE))
        scores = jnp.dot(q_rows, k_rows.T, preferred_element_type=jnp.float32) * scale
        scores = jnp.where(allowed, scores, -1e+30)
        top = lax.optimization_barrier(jnp.max(scores, axis=1, keepdims=True))
        probs = jnp.where(allowed, jnp.exp(scores - top), 0.0)
        weights = (probs / lax.optimization_barrier(jnp.sum(probs, axis=1, keepdims=True))).astype(jnp.bfloat16)
        return jnp.dot(weights, v_rows, preferred_element_type=jnp.float32)
    heads = lax.map(one_head, jnp.arange(QUERY_HEADS, dtype=jnp.int32))
    context = jnp.transpose(heads, (1, 0, 2)).reshape(PACKED_TOKENS, QUERY_HEADS * HEAD_SIZE).astype(jnp.bfloat16)
    wide = context.astype(jnp.float32)
    power = lax.optimization_barrier(jnp.mean(wide * wide, axis=1, keepdims=True))
    return (wide * gain.astype(jnp.float32) / jnp.sqrt(power + 1e-06)).astype(jnp.bfloat16)
```

```python
import functools
import math

import jax
import jax.numpy as jnp
from jax import lax
from jax.experimental import pallas as pl
from jax.experimental.pallas import tpu as pltpu
from jax.sharding import PartitionSpec as P

QUERY_HEADS = 96
HEAD_SIZE = 128
LOW = -1e31
MESH = pl.DeviceIdType.MESH
UNIT = 2


def attention_kernel(
    ctx_size, tp_size, back, ratio,
    query_ref, keys_ref, values_ref, lengths_ref,
    context_ref, inverse_ref,
    kv, q_v, out_v, lengths, cap, top, acc, squares, sums, sums_in,
    kv_sem, q_sem, len_sem, out_sem,
    recv_sem, fwd_sem, relay_sem, tp_send, tp_recv,
):
    rows = query_ref.shape[0]
    groups = keys_ref.shape[1] // HEAD_SIZE
    wide = ratio * HEAD_SIZE
    pairs = back // 2 + 1
    docs = lengths.shape[0]
    chips = ctx_size // 2
    me = lax.axis_index("ctx")
    my_tp = lax.axis_index("tp")
    chip = me // 2
    core = me % 2
    has_next = (chip + 1 < chips).astype(jnp.int32)
    factor = HEAD_SIZE ** (-0.5) * math.log2(math.e)

    def columns(g, width):
        return pl.ds(pl.multiple_of(g * width, width), width)

    def own_kv(g, which):
        src = (keys_ref, values_ref)[which]
        return pltpu.make_async_copy(
            src.at[:, columns(g, HEAD_SIZE)], kv.at[0, g, which], kv_sem.at[which, g]
        )

    def own_q(g):
        return pltpu.make_async_copy(query_ref.at[:, columns(g, wide)], q_v.at[g], q_sem.at[g])

    def write_out(g):
        return pltpu.make_async_copy(out_v.at[g], context_ref.at[:, columns(g, wide)], out_sem.at[g])

    own_lengths = pltpu.make_async_copy(lengths_ref, lengths, len_sem)

    for g in range(groups):
        own_kv(g, 0).start()
        own_kv(g, 1).start()
    own_lengths.start()
    for g in range(groups):
        own_q(g).start()

    barrier = pltpu.get_barrier_semaphore()

    def greet(ctx):
        pl.semaphore_signal(barrier, inc=1, device_id={"ctx": ctx}, device_id_type=MESH)

    greet(me + 1 - 2 * core)

    @pl.when(has_next == 1)
    def _():
        greet(me + 2)

    @pl.when(chip > 0)
    def _():
        greet(me - 2)

    @pl.when(core * has_next == 1)
    def _():
        greet(me + 1)

    @pl.when((1 - core) * chip > 0)
    def _():
        greet(me - 1)

    for o in range(1, tp_size):
        pl.semaphore_signal(
            barrier, inc=1, device_id={"tp": lax.rem(my_tp + o, tp_size)}, device_id_type=MESH
        )

    for d in range(1, 2 * pairs):
        def clear():
            kv[d] = jnp.zeros_like(kv[d])
        if d > back:
            clear()
        else:
            pl.when(me < d)(clear)

    own_lengths.wait()
    position = me * rows + lax.broadcasted_iota(jnp.int32, (rows, rows), 0)
    lane = lax.broadcasted_iota(jnp.int32, (rows, rows), 1)
    first = jnp.zeros((rows, rows), jnp.int32)
    end = jnp.int32(0)
    for i in range(docs):
        end = end + lengths[i]
        first = jnp.where(position >= end, end, first)
    for d in range(2 * pairs):
        key = (me - d) * rows + lane
        allowed = (key >= first) & (key <= position)
        cap[d // 2, :, (d % 2) * rows:(d % 2 + 1) * rows] = jnp.where(
            allowed, jnp.float32(jnp.inf), jnp.float32(LOW)
        )

    has_last = jnp.minimum(chip, 1)
    greeted = tp_size + has_next + has_last + core * has_next + (1 - core) * has_last
    pl.semaphore_wait(barrier, greeted)

    def send(src_slot, dst_slot, g, send_sem, ctx):
        return pltpu.make_async_remote_copy(
            src_ref=kv.at[src_slot, g],
            dst_ref=kv.at[dst_slot, g],
            send_sem=send_sem.at[src_slot // 2, g],
            recv_sem=recv_sem.at[dst_slot, g],
            device_id={"ctx": ctx},
            device_id_type=MESH,
        )

    def arrived(d, g):
        send(0, d, g, fwd_sem, me + 1 - 2 * core).wait_recv()

    def sends(e, g, act):
        if e + 2 <= back:
            @pl.when(has_next == 1)
            def _():
                act(send(e, e + 2, g, fwd_sem, me + 2))
        elif e + 1 <= back:
            @pl.when(core * has_next == 1)
            def _():
                act(send(e, e + 1, g, fwd_sem, me + 1))
        relay = send(e, e + 1 - 2 * core, g, relay_sem, me + 1 - 2 * core)
        if e == 0:
            pl.when(core == 0)(lambda: act(relay))
        elif e + 1 <= back:
            act(relay)
        else:
            pl.when(core == 1)(lambda: act(relay))

    def start(copy):
        copy.start()

    def finish(copy):
        copy.wait_send()

    def pass_on(g, carry):
        own_kv(g, 0).wait()
        own_kv(g, 1).wait()
        sends(0, g, start)
        return carry

    lax.fori_loop(0, groups, pass_on, 0)

    squares[...] = jnp.zeros_like(squares)

    def attend(j, g):
        k = jnp.concatenate([kv[2 * j, g, 0], kv[2 * j + 1, g, 0]], axis=0)
        v = jnp.concatenate([kv[2 * j, g, 1], kv[2 * j + 1, g, 1]], axis=0)
        v = jnp.concatenate([v, jnp.ones_like(v)], axis=1)
        for u in range(0, ratio, UNIT):
            heads = range(u, u + UNIT)
            q = jnp.concatenate(
                [q_v[g, :, h * HEAD_SIZE:(h + 1) * HEAD_SIZE] for h in heads], axis=0
            )
            s = lax.dot_general(
                q, k, (((1,), (1,)), ((), ())), preferred_element_type=jnp.float32
            )
            probs, tops, olds = [], [], []
            for n, h in enumerate(heads):
                part = jnp.minimum(s[n * rows:(n + 1) * rows], cap[j])
                high = jnp.broadcast_to(
                    jnp.max(part, axis=1, keepdims=True), (rows, HEAD_SIZE)
                )
                if j > 0:
                    old = top[g * ratio + h]
                    high = jnp.maximum(old, high)
                    olds.append(old)
                tops.append(high)
                both = jnp.concatenate([high, high], axis=1)
                probs.append(jnp.exp2((part - both) * factor).astype(jnp.bfloat16))
            update = jnp.dot(
                jnp.concatenate(probs, axis=0), v, preferred_element_type=jnp.float32
            )
            for n, h in enumerate(heads):
                at = g * ratio + h
                a = update[n * rows:(n + 1) * rows, :HEAD_SIZE]
                t = update[n * rows:(n + 1) * rows, HEAD_SIZE:]
                if j > 0:
                    correct = jnp.exp2((olds[n] - tops[n]) * factor)
                    a = a + acc[at, :, :HEAD_SIZE] * correct
                    t = t + acc[at, :, HEAD_SIZE:] * correct
                if j < pairs - 1:
                    top[at] = tops[n]
                    acc[at, :, :HEAD_SIZE] = a
                    acc[at, :, HEAD_SIZE:] = t
                else:
                    c = (a / t).astype(jnp.bfloat16)
                    out_v[g, :, h * HEAD_SIZE:(h + 1) * HEAD_SIZE] = c
                    c = c.astype(jnp.float32)
                    squares[...] += c * c

    for j in range(pairs):
        def step(g, carry):
            even, odd = 2 * j + 2, 2 * j + 1
            if even <= back:
                @pl.when(me >= even)
                def _():
                    arrived(even, g)
                    sends(even, g, start)
            if odd <= back:
                @pl.when(me >= odd)
                def _():
                    arrived(odd, g)
            if j == 0:
                own_q(g).wait()
            attend(j, g)
            if j == pairs - 1:
                write_out(g).start()
            return carry

        lax.fori_loop(0, groups, step, 0)

    mine = jnp.sum(squares[...].T, axis=0, keepdims=True)
    sums[...] = jnp.broadcast_to(mine, sums.shape)
    copies = []
    for o in range(1, tp_size):
        copies.append(pltpu.make_async_remote_copy(
            src_ref=sums,
            dst_ref=sums_in.at[o - 1],
            send_sem=tp_send.at[o - 1],
            recv_sem=tp_recv.at[o - 1],
            device_id={"tp": lax.rem(my_tp + o, tp_size)},
            device_id_type=MESH,
        ))
        copies[-1].start()

    def drain(g, carry):
        for e in range(0, back + 1, 2):
            if e == 0:
                sends(e, g, finish)
            else:
                pl.when(me >= e)(lambda: sends(e, g, finish))
        write_out(g).wait()
        return carry

    lax.fori_loop(0, groups, drain, 0)
    total = mine
    for o, copy in enumerate(copies):
        copy.wait()
        total = total + sums_in[o, 0:1, :]
    power = total / (QUERY_HEADS * HEAD_SIZE)
    inverse = 1.0 / jnp.sqrt(power + 1e-06)
    inverse_ref[...] = jnp.broadcast_to(inverse, (rows, rows)).T


def body(ctx_size, tp_size, query, keys, values, doc_lengths, gain):
    rows = query.shape[0]
    groups = keys.shape[1] // HEAD_SIZE
    heads = query.shape[1] // HEAD_SIZE
    ratio = heads // groups
    longest = rows * ctx_size * 5 // 8
    back = min(-(-(longest - 1) // rows), ctx_size - 1)
    pairs = back // 2 + 1
    context, inverse = pl.pallas_call(
        functools.partial(attention_kernel, ctx_size, tp_size, back, ratio),
        out_shape=(
            jax.ShapeDtypeStruct(query.shape, jnp.bfloat16),
            jax.ShapeDtypeStruct((rows, rows), jnp.float32),
        ),
        in_specs=[pl.BlockSpec(memory_space=pltpu.HBM)] * 4,
        out_specs=(
            pl.BlockSpec(memory_space=pl.ANY),
            pl.BlockSpec(memory_space=pltpu.VMEM),
        ),
        scratch_shapes=[
            pltpu.VMEM((2 * pairs, groups, 2, rows, HEAD_SIZE), jnp.bfloat16),
            pltpu.VMEM((groups, rows, ratio * HEAD_SIZE), jnp.bfloat16),
            pltpu.VMEM((groups, rows, ratio * HEAD_SIZE), jnp.bfloat16),
            pltpu.SMEM(doc_lengths.shape, jnp.int32),
            pltpu.VMEM((pairs, rows, 2 * rows), jnp.float32),
            pltpu.VMEM((heads, rows, HEAD_SIZE), jnp.float32),
            pltpu.VMEM((heads, rows, 2 * HEAD_SIZE), jnp.float32),
            pltpu.VMEM((rows, HEAD_SIZE), jnp.float32),
            pltpu.VMEM((8, rows), jnp.float32),
            pltpu.VMEM((tp_size, 8, rows), jnp.float32),
            pltpu.SemaphoreType.DMA((2, groups)),
            pltpu.SemaphoreType.DMA((groups,)),
            pltpu.SemaphoreType.DMA,
            pltpu.SemaphoreType.DMA((groups,)),
            pltpu.SemaphoreType.DMA((2 * pairs, groups)),
            pltpu.SemaphoreType.DMA((pairs, groups)),
            pltpu.SemaphoreType.DMA((pairs, groups)),
            pltpu.SemaphoreType.DMA((tp_size,)),
            pltpu.SemaphoreType.DMA((tp_size,)),
        ],
        compiler_params=pltpu.CompilerParams(
            collective_id=0, has_side_effects=True, vmem_limit_bytes=40 * 2**20
        ),
        cost_estimate=pl.CostEstimate(
            flops=4 * heads * rows * 2 * pairs * rows * HEAD_SIZE,
            bytes_accessed=4 * query.size + 4 * keys.size,
            transcendentals=heads * rows * 2 * pairs * rows,
        ),
    )(query, keys, values, doc_lengths)
    return (
        context.astype(jnp.float32) * gain.astype(jnp.float32)[None, :] * inverse[:, :1]
    ).astype(jnp.bfloat16)


def solution(mesh):
    return jax.shard_map(
        functools.partial(body, mesh.shape["ctx"], mesh.shape["tp"]),
        mesh=mesh,
        in_specs=(
            P(("dp", "ctx"), "tp"),
            P(("dp", "ctx"), "tp"),
            P(("dp", "ctx"), "tp"),
            P("dp"),
            P("tp"),
        ),
        out_specs=P(("dp", "ctx"), "tp"),
        check_vma=False,
    )
```

```python
import functools
import math

import jax
import jax.numpy as jnp
from jax import lax
from jax.experimental import pallas as pl
from jax.experimental.pallas import tpu as pltpu
from jax.sharding import PartitionSpec as P

QUERY_HEADS = 96
HEAD_SIZE = 128
LOW = -1e31
MESH = pl.DeviceIdType.MESH
UNIT = 4


def attention_kernel(
    ctx_size, tp_size, back, ratio,
    query_ref, keys_ref, values_ref, lengths_ref, gain_ref,
    context_ref, inverse_ref, wide_gain_ref,
    kv, own_keys, q_v, out_v, lengths, cap, top, acc, squares, sums, sums_in, gain_v, wide_gain_v, inverse_v,
    kv_sem, q_sem, len_sem, gain_sem, out_sem,
    recv_sem, fwd_sem, relay_sem, tp_send, tp_recv,
):
    rows = query_ref.shape[0]
    groups = keys_ref.shape[1] // HEAD_SIZE
    wide = ratio * HEAD_SIZE
    pairs = back // 2 + 1
    docs = lengths.shape[0]
    chips = ctx_size // 2
    me = lax.axis_index("ctx")
    my_tp = lax.axis_index("tp")
    chip = me // 2
    core = me % 2
    has_next = (chip + 1 < chips).astype(jnp.int32)
    factor = HEAD_SIZE ** (-0.5) * math.log2(math.e)

    def columns(g, width):
        return pl.ds(pl.multiple_of(g * width, width), width)

    def own_kv(g, which):
        src = (keys_ref, values_ref)[which]
        dst = (own_keys.at[g], kv.at[0, g, 1])[which]
        return pltpu.make_async_copy(src.at[:, columns(g, HEAD_SIZE)], dst, kv_sem.at[which, g])

    def own_q(g):
        return pltpu.make_async_copy(query_ref.at[:, columns(g, wide)], q_v.at[g], q_sem.at[g])

    def write_out(g):
        return pltpu.make_async_copy(out_v.at[g], context_ref.at[:, columns(g, wide)], out_sem.at[g])

    own_lengths = pltpu.make_async_copy(lengths_ref, lengths, len_sem)
    own_gain = pltpu.make_async_copy(gain_ref, gain_v, gain_sem.at[0])
    give_gain = pltpu.make_async_copy(wide_gain_v, wide_gain_ref, gain_sem.at[1])

    for g in range(groups):
        own_kv(g, 0).start()
        own_kv(g, 1).start()
    own_lengths.start()
    for g in range(groups):
        own_q(g).start()
    own_gain.start()

    barrier = pltpu.get_barrier_semaphore()

    def greet(ctx):
        pl.semaphore_signal(barrier, inc=1, device_id={"ctx": ctx}, device_id_type=MESH)

    greet(me + 1 - 2 * core)

    @pl.when(has_next == 1)
    def _():
        greet(me + 2)

    @pl.when(chip > 0)
    def _():
        greet(me - 2)

    @pl.when(core * has_next == 1)
    def _():
        greet(me + 1)

    @pl.when((1 - core) * chip > 0)
    def _():
        greet(me - 1)

    for o in range(1, tp_size):
        pl.semaphore_signal(
            barrier, inc=1, device_id={"tp": lax.rem(my_tp + o, tp_size)}, device_id_type=MESH
        )

    for d in range(1, 2 * pairs):
        def clear():
            kv[d] = jnp.zeros_like(kv[d])
        if d > back:
            clear()
        else:
            pl.when(me < d)(clear)

    own_lengths.wait()
    position = me * rows + lax.broadcasted_iota(jnp.int32, (rows, rows), 0)
    lane = lax.broadcasted_iota(jnp.int32, (rows, rows), 1)
    first = jnp.zeros((rows, rows), jnp.int32)
    end = jnp.int32(0)
    for i in range(docs):
        end = end + lengths[i]
        first = jnp.where(position >= end, end, first)
    for d in range(2 * pairs):
        key = (me - d) * rows + lane
        allowed = (key >= first) & (key <= position)
        cap[d // 2, :, (d % 2) * rows:(d % 2 + 1) * rows] = jnp.where(
            allowed, jnp.float32(jnp.inf), jnp.float32(LOW)
        )

    has_last = jnp.minimum(chip, 1)
    greeted = tp_size + has_next + has_last + core * has_next + (1 - core) * has_last

    for g in range(groups):
        own_kv(g, 0).wait()
        kv[0, g, 0] = own_keys[g].T
        own_kv(g, 1).wait()

    pl.semaphore_wait(barrier, greeted)

    def send(src_slot, dst_slot, g, send_sem, ctx):
        return pltpu.make_async_remote_copy(
            src_ref=kv.at[src_slot, g],
            dst_ref=kv.at[dst_slot, g],
            send_sem=send_sem.at[src_slot // 2, g],
            recv_sem=recv_sem.at[dst_slot, g],
            device_id={"ctx": ctx},
            device_id_type=MESH,
        )

    def arrived(d, g):
        send(0, d, g, fwd_sem, me + 1 - 2 * core).wait_recv()

    def sends(e, g, act):
        if e + 2 <= back:
            @pl.when(has_next == 1)
            def _():
                act(send(e, e + 2, g, fwd_sem, me + 2))
        elif e + 1 <= back:
            @pl.when(core * has_next == 1)
            def _():
                act(send(e, e + 1, g, fwd_sem, me + 1))
        relay = send(e, e + 1 - 2 * core, g, relay_sem, me + 1 - 2 * core)
        if e == 0:
            pl.when(core == 0)(lambda: act(relay))
        elif e + 1 <= back:
            act(relay)
        else:
            pl.when(core == 1)(lambda: act(relay))

    def start(copy):
        copy.start()

    def finish(copy):
        copy.wait_send()

    def pass_on(g, carry):
        sends(0, g, start)
        return carry

    lax.fori_loop(0, groups, pass_on, 0)

    squares[...] = jnp.zeros_like(squares)
    own_gain.wait()
    wide_gain_v[...] = gain_v[...].astype(jnp.float32)
    give_gain.start()

    def attend(j, g):
        k = jnp.concatenate([kv[2 * j, g, 0], kv[2 * j + 1, g, 0]], axis=1)
        v = jnp.concatenate([kv[2 * j, g, 1], kv[2 * j + 1, g, 1]], axis=0)
        v = jnp.concatenate([v, jnp.ones_like(v)], axis=1)
        first_head = g * ratio

        def scores(u):
            q = jnp.concatenate(
                [q_v[g, :, h * HEAD_SIZE:(h + 1) * HEAD_SIZE] for h in range(u, u + UNIT)], axis=0
            )
            return jnp.dot(q, k, preferred_element_type=jnp.float32)

        square = None
        following = scores(0)
        for u in range(0, ratio, UNIT):
            s = following
            if u + UNIT < ratio:
                following = scores(u + UNIT)
            olds, held = [], []
            if j > 0:
                olds = [top[first_head + u + n] for n in range(UNIT)]
                held = [acc[first_head + u + n] for n in range(UNIT)]
            probs, tops = [], []
            for n in range(UNIT):
                part = jnp.minimum(s[n * rows:(n + 1) * rows], cap[j])
                high = jnp.broadcast_to(
                    jnp.max(part, axis=1, keepdims=True), (rows, HEAD_SIZE)
                )
                if j > 0:
                    high = jnp.maximum(olds[n], high)
                tops.append(high)
                both = jnp.concatenate([high, high], axis=1)
                probs.append(jnp.exp2((part - both) * factor).astype(jnp.bfloat16))
            update = jnp.dot(
                jnp.concatenate(probs, axis=0), v, preferred_element_type=jnp.float32
            )
            for n in range(UNIT):
                at = update[n * rows:(n + 1) * rows]
                if j > 0:
                    correct = jnp.exp2((olds[n] - tops[n]) * factor)
                    at = at + held[n] * jnp.concatenate([correct, correct], axis=1)
                h = u + n
                if j < pairs - 1:
                    top[first_head + h] = tops[n]
                    acc[first_head + h] = at
                else:
                    c = (at[:, :HEAD_SIZE] / at[:, HEAD_SIZE:]).astype(jnp.bfloat16)
                    out_v[g, :, h * HEAD_SIZE:(h + 1) * HEAD_SIZE] = c
                    c = c.astype(jnp.float32)
                    square = c * c if square is None else square + c * c
        if square is not None:
            squares[...] += square

    for j in range(pairs):
        def step(g, carry):
            even, odd = 2 * j + 2, 2 * j + 1
            if even <= back:
                @pl.when(me >= even)
                def _():
                    arrived(even, g)
                    sends(even, g, start)
            if odd <= back:
                @pl.when(me >= odd)
                def _():
                    arrived(odd, g)
            if j == 0:
                own_q(g).wait()
            attend(j, g)
            if j == pairs - 1:
                write_out(g).start()
            return carry

        lax.fori_loop(0, groups, step, 0)

    mine = jnp.sum(squares[...].T, axis=0, keepdims=True)
    sums[...] = jnp.broadcast_to(mine, sums.shape)
    copies = []
    for o in range(1, tp_size):
        copies.append(pltpu.make_async_remote_copy(
            src_ref=sums,
            dst_ref=sums_in.at[o - 1],
            send_sem=tp_send.at[o - 1],
            recv_sem=tp_recv.at[o - 1],
            device_id={"tp": lax.rem(my_tp + o, tp_size)},
            device_id_type=MESH,
        ))
        copies[-1].start()

    def drain(g, carry):
        for e in range(0, back + 1, 2):
            if e == 0:
                sends(e, g, finish)
            else:
                pl.when(me >= e)(lambda: sends(e, g, finish))
        write_out(g).wait()
        return carry

    lax.fori_loop(0, groups, drain, 0)
    total = mine
    for o, copy in enumerate(copies):
        copy.wait()
        total = total + sums_in[o, 0:1, :]
    power = total / (QUERY_HEADS * HEAD_SIZE)
    inverse = 1.0 / jnp.sqrt(power + 1e-06)
    inverse_v[...] = jnp.broadcast_to(inverse, (rows, rows)).T
    give_inverse = pltpu.make_async_copy(inverse_v, inverse_ref, len_sem)
    give_inverse.start()
    give_gain.wait()
    give_inverse.wait()


def body(ctx_size, tp_size, query, keys, values, doc_lengths, gain):
    rows = query.shape[0]
    groups = keys.shape[1] // HEAD_SIZE
    heads = query.shape[1] // HEAD_SIZE
    ratio = heads // groups
    longest = rows * ctx_size * 5 // 8
    back = min(-(-(longest - 1) // rows), ctx_size - 1)
    pairs = back // 2 + 1
    gain_rows = gain.shape[0] // HEAD_SIZE
    context, inverse, wide_gain = pl.pallas_call(
        functools.partial(attention_kernel, ctx_size, tp_size, back, ratio),
        out_shape=(
            pltpu.VMEM(query.shape, jnp.bfloat16),
            pltpu.VMEM((rows, rows), jnp.float32),
            pltpu.VMEM((gain_rows, HEAD_SIZE), jnp.float32),
        ),
        in_specs=[pl.BlockSpec(memory_space=pltpu.HBM)] * 5,
        out_specs=(
            pl.BlockSpec(memory_space=pl.ANY),
            pl.BlockSpec(memory_space=pl.ANY),
            pl.BlockSpec(memory_space=pl.ANY),
        ),
        scratch_shapes=[
            pltpu.VMEM((2 * pairs, groups, 2, rows, HEAD_SIZE), jnp.bfloat16),
            pltpu.VMEM((groups, rows, HEAD_SIZE), jnp.bfloat16),
            pltpu.VMEM((groups, rows, ratio * HEAD_SIZE), jnp.bfloat16),
            pltpu.VMEM((groups, rows, ratio * HEAD_SIZE), jnp.bfloat16),
            pltpu.SMEM(doc_lengths.shape, jnp.int32),
            pltpu.VMEM((pairs, rows, 2 * rows), jnp.float32),
            pltpu.VMEM((heads, rows, HEAD_SIZE), jnp.float32),
            pltpu.VMEM((heads, rows, 2 * HEAD_SIZE), jnp.float32),
            pltpu.VMEM((rows, HEAD_SIZE), jnp.float32),
            pltpu.VMEM((8, rows), jnp.float32),
            pltpu.VMEM((tp_size, 8, rows), jnp.float32),
            pltpu.VMEM((gain_rows, HEAD_SIZE), jnp.bfloat16),
            pltpu.VMEM((gain_rows, HEAD_SIZE), jnp.float32),
            pltpu.VMEM((rows, rows), jnp.float32),
            pltpu.SemaphoreType.DMA((2, groups)),
            pltpu.SemaphoreType.DMA((groups,)),
            pltpu.SemaphoreType.DMA,
            pltpu.SemaphoreType.DMA((2,)),
            pltpu.SemaphoreType.DMA((groups,)),
            pltpu.SemaphoreType.DMA((2 * pairs, groups)),
            pltpu.SemaphoreType.DMA((pairs, groups)),
            pltpu.SemaphoreType.DMA((pairs, groups)),
            pltpu.SemaphoreType.DMA((tp_size,)),
            pltpu.SemaphoreType.DMA((tp_size,)),
        ],
        compiler_params=pltpu.CompilerParams(
            collective_id=0, has_side_effects=True, vmem_limit_bytes=56 * 2**20
        ),
        cost_estimate=pl.CostEstimate(
            flops=4 * heads * rows * 2 * pairs * rows * HEAD_SIZE,
            bytes_accessed=4 * query.size + 4 * keys.size,
            transcendentals=heads * rows * 2 * pairs * rows,
        ),
    )(query, keys, values, doc_lengths, gain.reshape(gain_rows, HEAD_SIZE))
    return (
        context.astype(jnp.float32) * wide_gain.reshape(1, -1) * inverse[:, :1]
    ).astype(jnp.bfloat16)


def solution(mesh):
    return jax.shard_map(
        functools.partial(body, mesh.shape["ctx"], mesh.shape["tp"]),
        mesh=mesh,
        in_specs=(
            P(("dp", "ctx"), "tp"),
            P(("dp", "ctx"), "tp"),
            P(("dp", "ctx"), "tp"),
            P("dp"),
            P("tp"),
        ),
        out_specs=P(("dp", "ctx"), "tp"),
        check_vma=False,
    )
```

```python
import functools
import math

import jax
import jax.numpy as jnp
from jax import lax
from jax.experimental import pallas as pl
from jax.experimental.pallas import tpu as pltpu
from jax.sharding import PartitionSpec as P

QUERY_HEADS = 96
HEAD_SIZE = 128
LOW = -1e31
MESH = pl.DeviceIdType.MESH
UNIT = 2
ONES = 16
AHEAD = 2


def attention_kernel(
    ctx_size, tp_size, back, ratio,
    query_ref, keys_ref, values_ref, lengths_ref, gain_ref,
    context_ref, inverse_ref, wide_gain_ref,
    kv, own_values, q_v, q_t, out_v, lengths, cap, top, acc, squares, sums, sums_in, gain_v, wide_gain_v, inverse_v,
    kv_sem, q_sem, len_sem, gain_sem, out_sem,
    recv_sem, fwd_sem, relay_sem, tp_send, tp_recv,
):
    rows = query_ref.shape[0]
    groups = keys_ref.shape[1] // HEAD_SIZE
    wide = ratio * HEAD_SIZE
    pairs = back // 2 + 1
    docs = lengths.shape[0]
    chips = ctx_size // 2
    me = lax.axis_index("ctx")
    my_tp = lax.axis_index("tp")
    chip = me // 2
    core = me % 2
    has_next = (chip + 1 < chips).astype(jnp.int32)
    factor = HEAD_SIZE ** (-0.5) * math.log2(math.e)

    def columns(g, width):
        return pl.ds(pl.multiple_of(g * width, width), width)

    def own_kv(g, which):
        src = (keys_ref, values_ref)[which]
        dst = (kv.at[0, g, 0], own_values.at[g])[which]
        return pltpu.make_async_copy(src.at[:, columns(g, HEAD_SIZE)], dst, kv_sem.at[which, g])

    def own_q(g):
        return pltpu.make_async_copy(query_ref.at[:, columns(g, wide)], q_v.at[g], q_sem.at[g])

    def write_out(g):
        return pltpu.make_async_copy(out_v.at[g], context_ref.at[:, columns(g, wide)], out_sem.at[g])

    own_lengths = pltpu.make_async_copy(lengths_ref, lengths, len_sem)
    own_gain = pltpu.make_async_copy(gain_ref, gain_v, gain_sem.at[0])
    give_gain = pltpu.make_async_copy(wide_gain_v, wide_gain_ref, gain_sem.at[1])

    for g in range(groups):
        own_kv(g, 0).start()
        own_kv(g, 1).start()
    own_lengths.start()
    for g in range(groups):
        own_q(g).start()
    own_gain.start()

    barrier = pltpu.get_barrier_semaphore()

    def greet(ctx):
        pl.semaphore_signal(barrier, inc=1, device_id={"ctx": ctx}, device_id_type=MESH)

    greet(me + 1 - 2 * core)

    @pl.when(has_next == 1)
    def _():
        greet(me + 2)

    @pl.when(chip > 0)
    def _():
        greet(me - 2)

    @pl.when(core * has_next == 1)
    def _():
        greet(me + 1)

    @pl.when((1 - core) * chip > 0)
    def _():
        greet(me - 1)

    for o in range(1, tp_size):
        pl.semaphore_signal(
            barrier, inc=1, device_id={"tp": lax.rem(my_tp + o, tp_size)}, device_id_type=MESH
        )

    for d in range(1, 2 * pairs):
        def clear():
            kv[d] = jnp.zeros_like(kv[d])
        if d > back:
            clear()
        else:
            pl.when(me < d)(clear)

    own_lengths.wait()
    position = me * rows + lax.broadcasted_iota(jnp.int32, (rows, rows), 1)
    offset = lax.broadcasted_iota(jnp.int32, (rows, rows), 0)
    first = jnp.zeros((rows, rows), jnp.int32)
    end = jnp.int32(0)
    for i in range(docs):
        end = end + lengths[i]
        first = jnp.where(position >= end, end, first)
    for d in range(2 * pairs):
        key = (me - d) * rows + offset
        allowed = (key >= first) & (key <= position)
        cap[d // 2, (d % 2) * rows:(d % 2 + 1) * rows, :] = jnp.where(
            allowed, jnp.float32(jnp.inf), jnp.float32(LOW)
        )

    has_last = jnp.minimum(chip, 1)
    greeted = tp_size + has_next + has_last + core * has_next + (1 - core) * has_last

    for g in range(groups):
        own_kv(g, 1).wait()
        kv[0, g, 1] = own_values[g].T
        own_kv(g, 0).wait()

    pl.semaphore_wait(barrier, greeted)

    def send(half, src_slot, dst_slot, g, send_sem, ctx):
        return pltpu.make_async_remote_copy(
            src_ref=kv.at[src_slot, g],
            dst_ref=kv.at[dst_slot, g],
            send_sem=send_sem.at[half, g],
            recv_sem=recv_sem.at[dst_slot, g],
            device_id={"ctx": ctx},
            device_id_type=MESH,
        )

    def arrived(d, g):
        send(0, 0, d, g, fwd_sem, me + 1 - 2 * core).wait_recv()

    def forward(n, act):
        half, g = n // groups, lax.rem(n, groups)
        e = 2 * half
        held = jnp.minimum(jnp.maximum(me - e + 1, 0), 1) * has_next

        @pl.when(held * jnp.minimum(jnp.maximum(back - e - 1, 0), 1) == 1)
        def _():
            act(send(half, e, e + 2, g, fwd_sem, me + 2))

        if back % 2 == 1:
            @pl.when((held * core == 1) & (e + 1 == back))
            def _():
                act(send(half, e, e + 1, g, fwd_sem, me + 1))

    def relay(e, g, act):
        copy = send(e // 2, e, e + 1 - 2 * core, g, relay_sem, me + 1 - 2 * core)
        if e == 0:
            pl.when(core == 0)(lambda: act(copy))
        elif e + 1 <= back:
            act(copy)
        else:
            pl.when(core == 1)(lambda: act(copy))

    def start(copy):
        copy.start()

    def finish(copy):
        copy.wait_send()

    for n in range(AHEAD):
        forward(jnp.int32(n), start)

    def pass_on(g, carry):
        relay(0, g, start)
        return carry

    lax.fori_loop(0, groups, pass_on, 0)

    def turn(g, carry):
        own_q(g).wait()
        for h in range(ratio):
            at = slice(h * HEAD_SIZE, (h + 1) * HEAD_SIZE)
            q_t[g, :, h * rows:(h + 1) * rows] = q_v[g, :, at].T
        return carry

    lax.fori_loop(0, groups, turn, 0)

    squares[...] = jnp.zeros_like(squares)
    own_gain.wait()
    wide_gain_v[...] = gain_v[...].astype(jnp.float32)
    give_gain.start()

    def attend(j, g):
        k = jnp.concatenate([kv[2 * j, g, 0], kv[2 * j + 1, g, 0]], axis=0)
        v = jnp.concatenate([kv[2 * j, g, 1], kv[2 * j + 1, g, 1]], axis=1)
        v = jnp.concatenate([v, jnp.ones((ONES, 2 * rows), v.dtype)], axis=0)
        first_head = g * ratio

        def scores(u):
            q = q_t[g, :, u * rows:(u + UNIT) * rows]
            return jnp.dot(k, q, preferred_element_type=jnp.float32)

        square = None
        following = scores(0)
        for u in range(0, ratio, UNIT):
            s = following
            if u + UNIT < ratio:
                following = scores(u + UNIT)
            olds, held = [], []
            if j > 0:
                olds = [top[first_head + u + n] for n in range(UNIT)]
                held = [acc[first_head + u + n] for n in range(UNIT)]
            probs, tops = [], []
            for n in range(UNIT):
                part = jnp.minimum(s[:, n * rows:(n + 1) * rows], cap[j])
                high = jnp.max(part, axis=0, keepdims=True)
                if j > 0:
                    high = jnp.maximum(olds[n], high)
                tops.append(high)
                probs.append(jnp.exp2((part - high) * factor).astype(jnp.bfloat16))
            update = jnp.dot(
                v, jnp.concatenate(probs, axis=1), preferred_element_type=jnp.float32
            )
            for n in range(UNIT):
                at = update[:, n * rows:(n + 1) * rows]
                if j > 0:
                    at = at + held[n] * jnp.exp2((olds[n] - tops[n]) * factor)
                h = u + n
                if j < pairs - 1:
                    top[first_head + h] = tops[n]
                    acc[first_head + h] = at
                else:
                    share = 1.0 / at[HEAD_SIZE:HEAD_SIZE + 1]
                    c = (at[:HEAD_SIZE] * share).astype(jnp.bfloat16)
                    out_v[g, :, h * HEAD_SIZE:(h + 1) * HEAD_SIZE] = c.T
                    c = c.astype(jnp.float32)
                    square = c * c if square is None else square + c * c
        if square is not None:
            squares[...] += square

    for j in range(pairs):
        def step(g, carry):
            even, odd = 2 * j + 2, 2 * j + 1
            if even <= back:
                @pl.when(me >= even)
                def _():
                    arrived(even, g)
                    relay(even, g, start)
            n = j * groups + g

            @pl.when(n + AHEAD < pairs * groups)
            def _():
                forward(n, finish)
                forward(n + AHEAD, start)

            if odd <= back:
                @pl.when(me >= odd)
                def _():
                    arrived(odd, g)
            attend(j, g)
            if j == pairs - 1:
                write_out(g).start()
            return carry

        lax.fori_loop(0, groups, step, 0)

    mine = jnp.sum(squares[...], axis=0, keepdims=True)
    sums[...] = jnp.broadcast_to(mine, sums.shape)
    copies = []
    for o in range(1, tp_size):
        copies.append(pltpu.make_async_remote_copy(
            src_ref=sums,
            dst_ref=sums_in.at[o - 1],
            send_sem=tp_send.at[o - 1],
            recv_sem=tp_recv.at[o - 1],
            device_id={"tp": lax.rem(my_tp + o, tp_size)},
            device_id_type=MESH,
        ))
        copies[-1].start()

    def drain(g, carry):
        for e in range(0, back + 1, 2):
            if e == 0:
                relay(e, g, finish)
            else:
                pl.when(me >= e)(lambda: relay(e, g, finish))
        write_out(g).wait()
        return carry

    lax.fori_loop(0, groups, drain, 0)
    for n in range(pairs * groups - AHEAD, pairs * groups):
        forward(jnp.int32(n), finish)
    total = mine
    for o, copy in enumerate(copies):
        copy.wait()
        total = total + sums_in[o, 0:1, :]
    power = total / (QUERY_HEADS * HEAD_SIZE)
    inverse = 1.0 / jnp.sqrt(power + 1e-06)
    inverse_v[...] = jnp.broadcast_to(inverse, (rows, rows)).T
    give_inverse = pltpu.make_async_copy(inverse_v, inverse_ref, len_sem)
    give_inverse.start()
    give_gain.wait()
    give_inverse.wait()


def body(ctx_size, tp_size, query, keys, values, doc_lengths, gain):
    rows = query.shape[0]
    groups = keys.shape[1] // HEAD_SIZE
    heads = query.shape[1] // HEAD_SIZE
    ratio = heads // groups
    longest = rows * ctx_size * 5 // 8
    back = min(-(-(longest - 1) // rows), ctx_size - 1)
    pairs = back // 2 + 1
    gain_rows = gain.shape[0] // HEAD_SIZE
    context, inverse, wide_gain = pl.pallas_call(
        functools.partial(attention_kernel, ctx_size, tp_size, back, ratio),
        out_shape=(
            pltpu.VMEM(query.shape, jnp.bfloat16),
            pltpu.VMEM((rows, rows), jnp.float32),
            pltpu.VMEM((gain_rows, HEAD_SIZE), jnp.float32),
        ),
        in_specs=[pl.BlockSpec(memory_space=pltpu.HBM)] * 5,
        out_specs=(
            pl.BlockSpec(memory_space=pl.ANY),
            pl.BlockSpec(memory_space=pl.ANY),
            pl.BlockSpec(memory_space=pl.ANY),
        ),
        scratch_shapes=[
            pltpu.VMEM((2 * pairs, groups, 2, rows, HEAD_SIZE), jnp.bfloat16),
            pltpu.VMEM((groups, rows, HEAD_SIZE), jnp.bfloat16),
            pltpu.VMEM((groups, rows, ratio * HEAD_SIZE), jnp.bfloat16),
            pltpu.VMEM((groups, HEAD_SIZE, ratio * rows), jnp.bfloat16),
            pltpu.VMEM((groups, rows, ratio * HEAD_SIZE), jnp.bfloat16),
            pltpu.SMEM(doc_lengths.shape, jnp.int32),
            pltpu.VMEM((pairs, 2 * rows, rows), jnp.float32),
            pltpu.VMEM((heads, 1, rows), jnp.float32),
            pltpu.VMEM((heads, HEAD_SIZE + ONES, rows), jnp.float32),
            pltpu.VMEM((HEAD_SIZE, rows), jnp.float32),
            pltpu.VMEM((8, rows), jnp.float32),
            pltpu.VMEM((tp_size, 8, rows), jnp.float32),
            pltpu.VMEM((gain_rows, HEAD_SIZE), jnp.bfloat16),
            pltpu.VMEM((gain_rows, HEAD_SIZE), jnp.float32),
            pltpu.VMEM((rows, rows), jnp.float32),
            pltpu.SemaphoreType.DMA((2, groups)),
            pltpu.SemaphoreType.DMA((groups,)),
            pltpu.SemaphoreType.DMA,
            pltpu.SemaphoreType.DMA((2,)),
            pltpu.SemaphoreType.DMA((groups,)),
            pltpu.SemaphoreType.DMA((2 * pairs, groups)),
            pltpu.SemaphoreType.DMA((pairs, groups)),
            pltpu.SemaphoreType.DMA((pairs, groups)),
            pltpu.SemaphoreType.DMA((tp_size,)),
            pltpu.SemaphoreType.DMA((tp_size,)),
        ],
        compiler_params=pltpu.CompilerParams(
            collective_id=0, has_side_effects=True, vmem_limit_bytes=56 * 2**20
        ),
        cost_estimate=pl.CostEstimate(
            flops=4 * heads * rows * 2 * pairs * rows * HEAD_SIZE,
            bytes_accessed=4 * query.size + 4 * keys.size,
            transcendentals=heads * rows * 2 * pairs * rows,
        ),
    )(query, keys, values, doc_lengths, gain.reshape(gain_rows, HEAD_SIZE))
    return (
        context.astype(jnp.float32) * wide_gain.reshape(1, -1) * inverse[:, :1]
    ).astype(jnp.bfloat16)


def solution(mesh):
    return jax.shard_map(
        functools.partial(body, mesh.shape["ctx"], mesh.shape["tp"]),
        mesh=mesh,
        in_specs=(
            P(("dp", "ctx"), "tp"),
            P(("dp", "ctx"), "tp"),
            P(("dp", "ctx"), "tp"),
            P("dp"),
            P("tp"),
        ),
        out_specs=P(("dp", "ctx"), "tp"),
        check_vma=False,
    )
```

```python
import functools
import math

import jax
import jax.numpy as jnp
from jax import lax
from jax.experimental import pallas as pl
from jax.experimental.pallas import tpu as pltpu
from jax.sharding import PartitionSpec as P

QUERY_HEADS = 96
HEAD_SIZE = 128
LOW = -1e31
MESH = pl.DeviceIdType.MESH
UNIT = 4
AHEAD = 2


def attention_kernel(
    ctx_size, tp_size, back, ratio,
    query_ref, keys_ref, values_ref, lengths_ref, gain_ref,
    context_ref, inverse_ref, wide_gain_ref,
    kv, own_keys, q_v, out_v, lengths, cap, top, acc, squares, sums, sums_in, gain_v, wide_gain_v, inverse_v,
    kv_sem, q_sem, len_sem, gain_sem, out_sem,
    recv_sem, fwd_sem, relay_sem, tp_send, tp_recv,
):
    rows = query_ref.shape[0]
    groups = keys_ref.shape[1] // HEAD_SIZE
    wide = ratio * HEAD_SIZE
    steps = [[0]] + [list(range(d, min(d + 2, back + 1))) for d in range(1, back + 1, 2)]
    chunks = (len(steps) - 1) * groups
    docs = lengths.shape[0]
    chips = ctx_size // 2
    me = lax.axis_index("ctx")
    my_tp = lax.axis_index("tp")
    chip = me // 2
    core = me % 2
    has_next = (chip + 1 < chips).astype(jnp.int32)
    factor = HEAD_SIZE ** (-0.5) * math.log2(math.e)

    def columns(g, width):
        return pl.ds(pl.multiple_of(g * width, width), width)

    def own_kv(g, which):
        src = (keys_ref, values_ref)[which]
        dst = (own_keys.at[g], kv.at[0, g, 1])[which]
        return pltpu.make_async_copy(src.at[:, columns(g, HEAD_SIZE)], dst, kv_sem.at[which, g])

    def own_q(g):
        return pltpu.make_async_copy(query_ref.at[:, columns(g, wide)], q_v.at[g], q_sem.at[g])

    def write_out(g):
        return pltpu.make_async_copy(out_v.at[g], context_ref.at[:, columns(g, wide)], out_sem.at[g])

    own_lengths = pltpu.make_async_copy(lengths_ref, lengths, len_sem)
    own_gain = pltpu.make_async_copy(gain_ref, gain_v, gain_sem.at[0])
    give_gain = pltpu.make_async_copy(wide_gain_v, wide_gain_ref, gain_sem.at[1])

    for g in range(groups):
        own_kv(g, 0).start()
        own_kv(g, 1).start()
    own_lengths.start()
    for g in range(groups):
        own_q(g).start()
    own_gain.start()

    barrier = pltpu.get_barrier_semaphore()

    def greet(ctx):
        pl.semaphore_signal(barrier, inc=1, device_id={"ctx": ctx}, device_id_type=MESH)

    greet(me + 1 - 2 * core)

    @pl.when(has_next == 1)
    def _():
        greet(me + 2)

    @pl.when(chip > 0)
    def _():
        greet(me - 2)

    @pl.when(core * has_next == 1)
    def _():
        greet(me + 1)

    @pl.when((1 - core) * chip > 0)
    def _():
        greet(me - 1)

    for o in range(1, tp_size):
        pl.semaphore_signal(
            barrier, inc=1, device_id={"tp": lax.rem(my_tp + o, tp_size)}, device_id_type=MESH
        )

    for d in range(1, back + 1):
        def clear():
            kv[d] = jnp.zeros_like(kv[d])
        pl.when(me < d)(clear)

    own_lengths.wait()
    position = me * rows + lax.broadcasted_iota(jnp.int32, (rows, rows), 0)
    offset = lax.broadcasted_iota(jnp.int32, (rows, rows), 1)
    first = jnp.zeros((rows, rows), jnp.int32)
    end = jnp.int32(0)
    for i in range(docs):
        end = end + lengths[i]
        first = jnp.where(position >= end, end, first)
    for d in range(back + 1):
        key = (me - d) * rows + offset
        allowed = (key >= first) & (key <= position)
        cap[d] = jnp.where(
            allowed, jnp.float32(jnp.inf), jnp.float32(LOW)
        )

    has_last = jnp.minimum(chip, 1)
    greeted = tp_size + has_next + has_last + core * has_next + (1 - core) * has_last

    for g in range(groups):
        own_kv(g, 0).wait()
        kv[0, g, 0] = own_keys[g].T
        own_kv(g, 1).wait()

    pl.semaphore_wait(barrier, greeted)

    def send(half, src_slot, dst_slot, g, send_sem, ctx):
        return pltpu.make_async_remote_copy(
            src_ref=kv.at[src_slot, g],
            dst_ref=kv.at[dst_slot, g],
            send_sem=send_sem.at[half, g],
            recv_sem=recv_sem.at[dst_slot, g],
            device_id={"ctx": ctx},
            device_id_type=MESH,
        )

    def arrived(d, g):
        send(0, 0, d, g, fwd_sem, me + 1 - 2 * core).wait_recv()

    def forward(n, act):
        half, g = n // groups, lax.rem(n, groups)
        e = 2 * half
        held = jnp.minimum(jnp.maximum(me - e + 1, 0), 1) * has_next

        @pl.when(held * jnp.minimum(jnp.maximum(back - e - 1, 0), 1) == 1)
        def _():
            act(send(half, e, e + 2, g, fwd_sem, me + 2))

        if back % 2 == 1:
            @pl.when((held * core == 1) & (e + 1 == back))
            def _():
                act(send(half, e, e + 1, g, fwd_sem, me + 1))

    def relay(e, g, act):
        copy = send(e // 2, e, e + 1 - 2 * core, g, relay_sem, me + 1 - 2 * core)
        if e == 0:
            pl.when(core == 0)(lambda: act(copy))
        elif e + 1 <= back:
            act(copy)
        else:
            pl.when(core == 1)(lambda: act(copy))

    def start(copy):
        copy.start()

    def finish(copy):
        copy.wait_send()

    for n in range(AHEAD):
        forward(jnp.int32(n), start)

    def pass_on(g, carry):
        relay(0, g, start)
        return carry

    lax.fori_loop(0, groups, pass_on, 0)

    squares[...] = jnp.zeros_like(squares)
    own_gain.wait()
    wide_gain_v[...] = gain_v[...].astype(jnp.float32)
    give_gain.start()

    def attend(j, g):
        slots = steps[j]
        k = jnp.concatenate([kv[d, g, 0] for d in slots], axis=1)
        v = jnp.concatenate([kv[d, g, 1] for d in slots], axis=0)
        v = jnp.concatenate([v, jnp.ones_like(v)], axis=1)
        limit = jnp.concatenate([cap[d] for d in slots], axis=1)
        first_head = g * ratio

        def scores(u):
            q = jnp.concatenate(
                [q_v[g, :, h * HEAD_SIZE:(h + 1) * HEAD_SIZE] for h in range(u, u + UNIT)], axis=0
            )
            return jnp.dot(q, k, preferred_element_type=jnp.float32)

        square = None
        following = scores(0)
        for u in range(0, ratio, UNIT):
            s = following
            if u + UNIT < ratio:
                following = scores(u + UNIT)
            olds, held = [], []
            if j > 0:
                olds = [top[first_head + u + n] for n in range(UNIT)]
                held = [acc[first_head + u + n] for n in range(UNIT)]
            probs, tops = [], []
            for n in range(UNIT):
                part = jnp.minimum(s[n * rows:(n + 1) * rows], limit)
                high = jnp.broadcast_to(
                    jnp.max(part, axis=1, keepdims=True), (rows, HEAD_SIZE)
                )
                if j > 0:
                    high = jnp.maximum(olds[n], high)
                tops.append(high)
                wide_high = jnp.concatenate([high] * len(slots), axis=1)
                probs.append(jnp.exp2((part - wide_high) * factor).astype(jnp.bfloat16))
            update = jnp.dot(
                jnp.concatenate(probs, axis=0), v, preferred_element_type=jnp.float32
            )
            for n in range(UNIT):
                at = update[n * rows:(n + 1) * rows]
                if j > 0:
                    correct = jnp.exp2((olds[n] - tops[n]) * factor)
                    at = at + held[n] * jnp.concatenate([correct, correct], axis=1)
                h = u + n
                if j < len(steps) - 1:
                    top[first_head + h] = tops[n]
                    acc[first_head + h] = at
                else:
                    c = (at[:, :HEAD_SIZE] / at[:, HEAD_SIZE:]).astype(jnp.bfloat16)
                    out_v[g, :, h * HEAD_SIZE:(h + 1) * HEAD_SIZE] = c
                    c = c.astype(jnp.float32)
                    square = c * c if square is None else square + c * c
        if square is not None:
            squares[...] += square

    for j in range(len(steps)):
        def step(g, carry):
            if j == 0:
                own_q(g).wait()
            else:
                odd, even = 2 * j - 1, 2 * j
                if even <= back:
                    @pl.when(me >= even)
                    def _():
                        arrived(even, g)
                        relay(even, g, start)
                n = (j - 1) * groups + g

                @pl.when(n + AHEAD < chunks)
                def _():
                    forward(n, finish)
                    forward(n + AHEAD, start)

                @pl.when(me >= odd)
                def _():
                    arrived(odd, g)
            attend(j, g)
            if j == len(steps) - 1:
                write_out(g).start()
            return carry

        lax.fori_loop(0, groups, step, 0)

    mine = jnp.sum(squares[...].T, axis=0, keepdims=True)
    sums[...] = jnp.broadcast_to(mine, sums.shape)
    copies = []
    for o in range(1, tp_size):
        copies.append(pltpu.make_async_remote_copy(
            src_ref=sums,
            dst_ref=sums_in.at[o - 1],
            send_sem=tp_send.at[o - 1],
            recv_sem=tp_recv.at[o - 1],
            device_id={"tp": lax.rem(my_tp + o, tp_size)},
            device_id_type=MESH,
        ))
        copies[-1].start()

    def drain(g, carry):
        for e in range(0, back + 1, 2):
            if e == 0:
                relay(e, g, finish)
            else:
                pl.when(me >= e)(lambda: relay(e, g, finish))
        write_out(g).wait()
        return carry

    lax.fori_loop(0, groups, drain, 0)
    for n in range(chunks - AHEAD, chunks):
        forward(jnp.int32(n), finish)
    total = mine
    for o, copy in enumerate(copies):
        copy.wait()
        total = total + sums_in[o, 0:1, :]
    power = total / (QUERY_HEADS * HEAD_SIZE)
    inverse = 1.0 / jnp.sqrt(power + 1e-06)
    inverse_v[...] = jnp.broadcast_to(inverse, (rows, rows)).T
    give_inverse = pltpu.make_async_copy(inverse_v, inverse_ref, len_sem)
    give_inverse.start()
    give_gain.wait()
    give_inverse.wait()


def body(ctx_size, tp_size, query, keys, values, doc_lengths, gain):
    rows = query.shape[0]
    groups = keys.shape[1] // HEAD_SIZE
    heads = query.shape[1] // HEAD_SIZE
    ratio = heads // groups
    longest = rows * ctx_size * 5 // 8
    back = min(-(-(longest - 1) // rows), ctx_size - 1)
    halves = back // 2 + 1
    gain_rows = gain.shape[0] // HEAD_SIZE
    context, inverse, wide_gain = pl.pallas_call(
        functools.partial(attention_kernel, ctx_size, tp_size, back, ratio),
        out_shape=(
            pltpu.VMEM(query.shape, jnp.bfloat16),
            pltpu.VMEM((rows, rows), jnp.float32),
            pltpu.VMEM((gain_rows, HEAD_SIZE), jnp.float32),
        ),
        in_specs=[pl.BlockSpec(memory_space=pltpu.HBM)] * 5,
        out_specs=(
            pl.BlockSpec(memory_space=pl.ANY),
            pl.BlockSpec(memory_space=pl.ANY),
            pl.BlockSpec(memory_space=pl.ANY),
        ),
        scratch_shapes=[
            pltpu.VMEM((back + 1, groups, 2, rows, HEAD_SIZE), jnp.bfloat16),
            pltpu.VMEM((groups, rows, HEAD_SIZE), jnp.bfloat16),
            pltpu.VMEM((groups, rows, ratio * HEAD_SIZE), jnp.bfloat16),
            pltpu.VMEM((groups, rows, ratio * HEAD_SIZE), jnp.bfloat16),
            pltpu.SMEM(doc_lengths.shape, jnp.int32),
            pltpu.VMEM((back + 1, rows, rows), jnp.float32),
            pltpu.VMEM((heads, rows, HEAD_SIZE), jnp.float32),
            pltpu.VMEM((heads, rows, 2 * HEAD_SIZE), jnp.float32),
            pltpu.VMEM((rows, HEAD_SIZE), jnp.float32),
            pltpu.VMEM((8, rows), jnp.float32),
            pltpu.VMEM((tp_size, 8, rows), jnp.float32),
            pltpu.VMEM((gain_rows, HEAD_SIZE), jnp.bfloat16),
            pltpu.VMEM((gain_rows, HEAD_SIZE), jnp.float32),
            pltpu.VMEM((rows, rows), jnp.float32),
            pltpu.SemaphoreType.DMA((2, groups)),
            pltpu.SemaphoreType.DMA((groups,)),
            pltpu.SemaphoreType.DMA,
            pltpu.SemaphoreType.DMA((2,)),
            pltpu.SemaphoreType.DMA((groups,)),
            pltpu.SemaphoreType.DMA((back + 1, groups)),
            pltpu.SemaphoreType.DMA((halves, groups)),
            pltpu.SemaphoreType.DMA((halves, groups)),
            pltpu.SemaphoreType.DMA((tp_size,)),
            pltpu.SemaphoreType.DMA((tp_size,)),
        ],
        compiler_params=pltpu.CompilerParams(
            collective_id=0, has_side_effects=True, vmem_limit_bytes=56 * 2**20
        ),
        cost_estimate=pl.CostEstimate(
            flops=4 * heads * rows * (back + 1) * rows * HEAD_SIZE,
            bytes_accessed=4 * query.size + 4 * keys.size,
            transcendentals=heads * rows * (back + 1) * rows,
        ),
    )(query, keys, values, doc_lengths, gain.reshape(gain_rows, HEAD_SIZE))
    return (
        context.astype(jnp.float32) * wide_gain.reshape(1, -1) * inverse[:, :1]
    ).astype(jnp.bfloat16)


def solution(mesh):
    return jax.shard_map(
        functools.partial(body, mesh.shape["ctx"], mesh.shape["tp"]),
        mesh=mesh,
        in_specs=(
            P(("dp", "ctx"), "tp"),
            P(("dp", "ctx"), "tp"),
            P(("dp", "ctx"), "tp"),
            P("dp"),
            P("tp"),
        ),
        out_specs=P(("dp", "ctx"), "tp"),
        check_vma=False,
    )
```

```python
import functools
import math

import jax
import jax.numpy as jnp
from jax import lax
from jax.experimental import pallas as pl
from jax.experimental.pallas import tpu as pltpu
from jax.sharding import PartitionSpec as P

QUERY_HEADS = 96
HEAD_SIZE = 128
LOW = -1e31
MESH = pl.DeviceIdType.MESH
UNIT = 12
AHEAD = 2


def attention_kernel(
    ctx_size, tp_size, back, ratio,
    query_ref, keys_ref, values_ref, lengths_ref, gain_ref,
    context_ref, inverse_ref, wide_gain_ref,
    kv, own_keys, q_v, out_v, lengths, cap, top, acc, squares, sums, sums_in, gain_v, wide_gain_v, inverse_v,
    kv_sem, q_sem, len_sem, gain_sem, out_sem,
    recv_sem, fwd_sem, relay_sem, tp_send, tp_recv,
):
    rows = query_ref.shape[0]
    groups = keys_ref.shape[1] // HEAD_SIZE
    wide = ratio * HEAD_SIZE
    steps = [list(range(d, min(d + 2, back + 1))) for d in range(0, back + 1, 2)]
    chunks = (back + 1) // 2 * groups
    docs = lengths.shape[0]
    chips = ctx_size // 2
    me = lax.axis_index("ctx")
    my_tp = lax.axis_index("tp")
    chip = me // 2
    core = me % 2
    has_next = (chip + 1 < chips).astype(jnp.int32)
    factor = HEAD_SIZE ** (-0.5) * math.log2(math.e)

    def columns(g, width):
        return pl.ds(pl.multiple_of(g * width, width), width)

    def own_kv(g, which):
        src = (keys_ref, values_ref)[which]
        dst = (own_keys.at[g], kv.at[0, g, 1])[which]
        return pltpu.make_async_copy(src.at[:, columns(g, HEAD_SIZE)], dst, kv_sem.at[which, g])

    def own_q(g):
        return pltpu.make_async_copy(query_ref.at[:, columns(g, wide)], q_v.at[g], q_sem.at[g])

    def write_out(g):
        return pltpu.make_async_copy(out_v.at[g], context_ref.at[:, columns(g, wide)], out_sem.at[g])

    own_lengths = pltpu.make_async_copy(lengths_ref, lengths, len_sem)
    own_gain = pltpu.make_async_copy(gain_ref, gain_v, gain_sem.at[0])
    give_gain = pltpu.make_async_copy(wide_gain_v, wide_gain_ref, gain_sem.at[1])

    for g in range(groups):
        own_kv(g, 0).start()
        own_kv(g, 1).start()
    own_lengths.start()
    for g in range(groups):
        own_q(g).start()
    own_gain.start()

    barrier = pltpu.get_barrier_semaphore()

    def greet(ctx):
        pl.semaphore_signal(barrier, inc=1, device_id={"ctx": ctx}, device_id_type=MESH)

    greet(me + 1 - 2 * core)

    @pl.when(has_next == 1)
    def _():
        greet(me + 2)

    @pl.when(chip > 0)
    def _():
        greet(me - 2)

    @pl.when(core * has_next == 1)
    def _():
        greet(me + 1)

    @pl.when((1 - core) * chip > 0)
    def _():
        greet(me - 1)

    for o in range(1, tp_size):
        pl.semaphore_signal(
            barrier, inc=1, device_id={"tp": lax.rem(my_tp + o, tp_size)}, device_id_type=MESH
        )

    for d in range(1, back + 1):
        def clear():
            kv[d] = jnp.zeros_like(kv[d])
        pl.when(me < d)(clear)

    own_lengths.wait()
    position = me * rows + lax.broadcasted_iota(jnp.int32, (rows, rows), 0)
    offset = lax.broadcasted_iota(jnp.int32, (rows, rows), 1)
    first = jnp.zeros((rows, rows), jnp.int32)
    end = jnp.int32(0)
    for i in range(docs):
        end = end + lengths[i]
        first = jnp.where(position >= end, end, first)
    for d in range(back + 1):
        key = (me - d) * rows + offset
        allowed = (key >= first) & (key <= position)
        cap[d] = jnp.where(
            allowed, jnp.float32(jnp.inf), jnp.float32(LOW)
        )

    has_last = jnp.minimum(chip, 1)
    greeted = tp_size + has_next + has_last + core * has_next + (1 - core) * has_last

    for g in range(groups):
        own_kv(g, 0).wait()
        kv[0, g, 0] = own_keys[g].T
        own_kv(g, 1).wait()

    pl.semaphore_wait(barrier, greeted)

    def send(half, src_slot, dst_slot, g, send_sem, ctx):
        return pltpu.make_async_remote_copy(
            src_ref=kv.at[src_slot, g],
            dst_ref=kv.at[dst_slot, g],
            send_sem=send_sem.at[half, g],
            recv_sem=recv_sem.at[dst_slot, g],
            device_id={"ctx": ctx},
            device_id_type=MESH,
        )

    def arrived(d, g):
        send(0, 0, d, g, fwd_sem, me + 1 - 2 * core).wait_recv()

    def forward(n, act):
        half, g = n // groups, lax.rem(n, groups)
        e = 2 * half
        held = jnp.minimum(jnp.maximum(me - e + 1, 0), 1) * has_next

        @pl.when(held * jnp.minimum(jnp.maximum(back - e - 1, 0), 1) == 1)
        def _():
            act(send(half, e, e + 2, g, fwd_sem, me + 2))

        if back % 2 == 1:
            @pl.when((held * core == 1) & (e + 1 == back))
            def _():
                act(send(half, e, e + 1, g, fwd_sem, me + 1))

    def relay(e, g, act):
        copy = send(e // 2, e, e + 1 - 2 * core, g, relay_sem, me + 1 - 2 * core)
        if e == 0:
            pl.when(core == 0)(lambda: act(copy))
        elif e + 1 <= back:
            act(copy)
        else:
            pl.when(core == 1)(lambda: act(copy))

    def start(copy):
        copy.start()

    def finish(copy):
        copy.wait_send()

    for n in range(AHEAD):
        forward(jnp.int32(n), start)

    def pass_on(g, carry):
        relay(0, g, start)
        return carry

    lax.fori_loop(0, groups, pass_on, 0)

    squares[...] = jnp.zeros_like(squares)
    own_gain.wait()
    wide_gain_v[...] = gain_v[...].astype(jnp.float32)
    give_gain.start()

    def attend(j, g):
        slots = steps[j]
        k = jnp.concatenate([kv[d, g, 0] for d in slots], axis=1)
        v = jnp.concatenate([kv[d, g, 1] for d in slots], axis=0)
        v = jnp.concatenate([v, jnp.ones_like(v)], axis=1)
        limit = jnp.concatenate([cap[d] for d in slots], axis=1)
        first_head = g * ratio

        def scores(u):
            q = jnp.concatenate(
                [q_v[g, :, h * HEAD_SIZE:(h + 1) * HEAD_SIZE] for h in range(u, u + UNIT)], axis=0
            )
            return jnp.dot(q, k, preferred_element_type=jnp.float32)

        square = None
        following = scores(0)
        for u in range(0, ratio, UNIT):
            s = following
            if u + UNIT < ratio:
                following = scores(u + UNIT)
            olds, held = [], []
            if j > 0:
                olds = [top[first_head + u + n] for n in range(UNIT)]
                held = [acc[first_head + u + n] for n in range(UNIT)]
            probs, tops = [], []
            for n in range(UNIT):
                part = jnp.minimum(s[n * rows:(n + 1) * rows], limit)
                high = jnp.broadcast_to(
                    jnp.max(part, axis=1, keepdims=True), (rows, HEAD_SIZE)
                )
                if j > 0:
                    high = jnp.maximum(olds[n], high)
                tops.append(high)
                wide_high = jnp.concatenate([high] * len(slots), axis=1)
                probs.append(jnp.exp2((part - wide_high) * factor).astype(jnp.bfloat16))
            update = jnp.dot(
                jnp.concatenate(probs, axis=0), v, preferred_element_type=jnp.float32
            )
            for n in range(UNIT):
                at = update[n * rows:(n + 1) * rows]
                if j > 0:
                    correct = jnp.exp2((olds[n] - tops[n]) * factor)
                    at = at + held[n] * jnp.concatenate([correct, correct], axis=1)
                h = u + n
                if j < len(steps) - 1:
                    top[first_head + h] = tops[n]
                    acc[first_head + h] = at
                else:
                    c = (at[:, :HEAD_SIZE] / at[:, HEAD_SIZE:]).astype(jnp.bfloat16)
                    out_v[g, :, h * HEAD_SIZE:(h + 1) * HEAD_SIZE] = c
                    c = c.astype(jnp.float32)
                    square = c * c if square is None else square + c * c
        if square is not None:
            squares[...] += square

    for j in range(len(steps)):
        def step(g, carry):
            even, odd = 2 * j + 2, 2 * j + 1
            if even <= back:
                @pl.when(me >= even)
                def _():
                    arrived(even, g)
                    relay(even, g, start)
            n = j * groups + g

            @pl.when(n + AHEAD < chunks)
            def _():
                forward(n, finish)
                forward(n + AHEAD, start)

            if odd <= back:
                @pl.when(me >= odd)
                def _():
                    arrived(odd, g)
            if j == 0:
                own_q(g).wait()
            attend(j, g)
            if j == len(steps) - 1:
                write_out(g).start()
            return carry

        lax.fori_loop(0, groups, step, 0)

    mine = jnp.sum(squares[...].T, axis=0, keepdims=True)
    sums[...] = jnp.broadcast_to(mine, sums.shape)
    copies = []
    for o in range(1, tp_size):
        copies.append(pltpu.make_async_remote_copy(
            src_ref=sums,
            dst_ref=sums_in.at[o - 1],
            send_sem=tp_send.at[o - 1],
            recv_sem=tp_recv.at[o - 1],
            device_id={"tp": lax.rem(my_tp + o, tp_size)},
            device_id_type=MESH,
        ))
        copies[-1].start()

    def drain(g, carry):
        for e in range(0, back + 1, 2):
            if e == 0:
                relay(e, g, finish)
            else:
                pl.when(me >= e)(lambda: relay(e, g, finish))
        write_out(g).wait()
        return carry

    lax.fori_loop(0, groups, drain, 0)
    for n in range(chunks - AHEAD, chunks):
        forward(jnp.int32(n), finish)
    total = mine
    for o, copy in enumerate(copies):
        copy.wait()
        total = total + sums_in[o, 0:1, :]
    power = total / (QUERY_HEADS * HEAD_SIZE)
    inverse = 1.0 / jnp.sqrt(power + 1e-06)
    inverse_v[...] = jnp.broadcast_to(inverse, (rows, rows)).T
    give_inverse = pltpu.make_async_copy(inverse_v, inverse_ref, len_sem)
    give_inverse.start()
    give_gain.wait()
    give_inverse.wait()


def body(ctx_size, tp_size, query, keys, values, doc_lengths, gain):
    rows = query.shape[0]
    groups = keys.shape[1] // HEAD_SIZE
    heads = query.shape[1] // HEAD_SIZE
    ratio = heads // groups
    longest = rows * ctx_size * 5 // 8
    back = min(-(-(longest - 1) // rows), ctx_size - 1)
    halves = back // 2 + 1
    gain_rows = gain.shape[0] // HEAD_SIZE
    context, inverse, wide_gain = pl.pallas_call(
        functools.partial(attention_kernel, ctx_size, tp_size, back, ratio),
        out_shape=(
            pltpu.VMEM(query.shape, jnp.bfloat16),
            pltpu.VMEM((rows, rows), jnp.float32),
            pltpu.VMEM((gain_rows, HEAD_SIZE), jnp.float32),
        ),
        in_specs=[pl.BlockSpec(memory_space=pltpu.HBM)] * 5,
        out_specs=(
            pl.BlockSpec(memory_space=pl.ANY),
            pl.BlockSpec(memory_space=pl.ANY),
            pl.BlockSpec(memory_space=pl.ANY),
        ),
        scratch_shapes=[
            pltpu.VMEM((back + 1, groups, 2, rows, HEAD_SIZE), jnp.bfloat16),
            pltpu.VMEM((groups, rows, HEAD_SIZE), jnp.bfloat16),
            pltpu.VMEM((groups, rows, ratio * HEAD_SIZE), jnp.bfloat16),
            pltpu.VMEM((groups, rows, ratio * HEAD_SIZE), jnp.bfloat16),
            pltpu.SMEM(doc_lengths.shape, jnp.int32),
            pltpu.VMEM((back + 1, rows, rows), jnp.float32),
            pltpu.VMEM((heads, rows, HEAD_SIZE), jnp.float32),
            pltpu.VMEM((heads, rows, 2 * HEAD_SIZE), jnp.float32),
            pltpu.VMEM((rows, HEAD_SIZE), jnp.float32),
            pltpu.VMEM((8, rows), jnp.float32),
            pltpu.VMEM((tp_size, 8, rows), jnp.float32),
            pltpu.VMEM((gain_rows, HEAD_SIZE), jnp.bfloat16),
            pltpu.VMEM((gain_rows, HEAD_SIZE), jnp.float32),
            pltpu.VMEM((rows, rows), jnp.float32),
            pltpu.SemaphoreType.DMA((2, groups)),
            pltpu.SemaphoreType.DMA((groups,)),
            pltpu.SemaphoreType.DMA,
            pltpu.SemaphoreType.DMA((2,)),
            pltpu.SemaphoreType.DMA((groups,)),
            pltpu.SemaphoreType.DMA((back + 1, groups)),
            pltpu.SemaphoreType.DMA((halves, groups)),
            pltpu.SemaphoreType.DMA((halves, groups)),
            pltpu.SemaphoreType.DMA((tp_size,)),
            pltpu.SemaphoreType.DMA((tp_size,)),
        ],
        compiler_params=pltpu.CompilerParams(
            collective_id=0, has_side_effects=True, vmem_limit_bytes=56 * 2**20
        ),
        cost_estimate=pl.CostEstimate(
            flops=4 * heads * rows * (back + 1) * rows * HEAD_SIZE,
            bytes_accessed=4 * query.size + 4 * keys.size,
            transcendentals=heads * rows * (back + 1) * rows,
        ),
    )(query, keys, values, doc_lengths, gain.reshape(gain_rows, HEAD_SIZE))
    return (
        context.astype(jnp.float32) * wide_gain.reshape(1, -1) * inverse[:, :1]
    ).astype(jnp.bfloat16)


def solution(mesh):
    return jax.shard_map(
        functools.partial(body, mesh.shape["ctx"], mesh.shape["tp"]),
        mesh=mesh,
        in_specs=(
            P(("dp", "ctx"), "tp"),
            P(("dp", "ctx"), "tp"),
            P(("dp", "ctx"), "tp"),
            P("dp"),
            P("tp"),
        ),
        out_specs=P(("dp", "ctx"), "tp"),
        check_vma=False,
    )
```

```python
import functools
import math

import jax
import jax.numpy as jnp
from jax import lax
from jax.experimental import pallas as pl
from jax.experimental.pallas import tpu as pltpu
from jax.sharding import PartitionSpec as P

QUERY_HEADS = 96
HEAD_SIZE = 128
LOW = -1e31
MESH = pl.DeviceIdType.MESH
UNIT = 4
AHEAD = 3


def attention_kernel(
    ctx_size, tp_size, back, ratio,
    query_ref, keys_ref, values_ref, lengths_ref, gain_ref,
    context_ref, inverse_ref, wide_gain_ref,
    kv, own_keys, q_v, out_v, lengths, cap, top, acc, squares, sums, sums_in, gain_v, wide_gain_v, inverse_v,
    kv_sem, q_sem, len_sem, gain_sem, out_sem,
    recv_sem, fwd_sem, relay_sem, tp_send, tp_recv,
):
    rows = query_ref.shape[0]
    groups = keys_ref.shape[1] // HEAD_SIZE
    wide = ratio * HEAD_SIZE
    steps = [[0]] + [list(range(d, min(d + 2, back + 1))) for d in range(1, back + 1, 2)]
    chunks = (len(steps) - 1) * groups
    ahead = min(AHEAD, groups)
    docs = lengths.shape[0]
    chips = ctx_size // 2
    me = lax.axis_index("ctx")
    my_tp = lax.axis_index("tp")
    chip = me // 2
    core = me % 2
    has_next = (chip + 1 < chips).astype(jnp.int32)
    factor = HEAD_SIZE ** (-0.5) * math.log2(math.e)

    def columns(g, width):
        return pl.ds(pl.multiple_of(g * width, width), width)

    def own_kv(g, which):
        src = (keys_ref, values_ref)[which]
        dst = (own_keys.at[g], kv.at[0, g, 1])[which]
        return pltpu.make_async_copy(src.at[:, columns(g, HEAD_SIZE)], dst, kv_sem.at[which, g])

    def own_q(g):
        return pltpu.make_async_copy(query_ref.at[:, columns(g, wide)], q_v.at[g], q_sem.at[g])

    def write_out(g):
        return pltpu.make_async_copy(out_v.at[g], context_ref.at[:, columns(g, wide)], out_sem.at[g])

    own_lengths = pltpu.make_async_copy(lengths_ref, lengths, len_sem)
    own_gain = pltpu.make_async_copy(gain_ref, gain_v, gain_sem.at[0])
    give_gain = pltpu.make_async_copy(wide_gain_v, wide_gain_ref, gain_sem.at[1])

    for g in range(groups):
        own_kv(g, 0).start()
        own_kv(g, 1).start()
    own_lengths.start()
    for g in range(groups):
        own_q(g).start()
    own_gain.start()

    barrier = pltpu.get_barrier_semaphore()

    def greet(ctx):
        pl.semaphore_signal(barrier, inc=1, device_id={"ctx": ctx}, device_id_type=MESH)

    greet(me + 1 - 2 * core)

    @pl.when(has_next == 1)
    def _():
        greet(me + 2)

    @pl.when(chip > 0)
    def _():
        greet(me - 2)

    @pl.when(core * has_next == 1)
    def _():
        greet(me + 1)

    @pl.when((1 - core) * chip > 0)
    def _():
        greet(me - 1)

    for o in range(1, tp_size):
        pl.semaphore_signal(
            barrier, inc=1, device_id={"tp": lax.rem(my_tp + o, tp_size)}, device_id_type=MESH
        )

    for d in range(1, back + 1):
        def clear():
            kv[d] = jnp.zeros_like(kv[d])
        pl.when(me < d)(clear)

    own_lengths.wait()
    position = me * rows + lax.broadcasted_iota(jnp.int32, (rows, rows), 0)
    offset = lax.broadcasted_iota(jnp.int32, (rows, rows), 1)
    first = jnp.zeros((rows, rows), jnp.int32)
    end = jnp.int32(0)
    for i in range(docs):
        end = end + lengths[i]
        first = jnp.where(position >= end, end, first)
    for d in range(back + 1):
        key = (me - d) * rows + offset
        allowed = (key >= first) & (key <= position)
        cap[d] = jnp.where(
            allowed, jnp.float32(jnp.inf), jnp.float32(LOW)
        )

    has_last = jnp.minimum(chip, 1)
    greeted = tp_size + has_next + has_last + core * has_next + (1 - core) * has_last

    for g in range(groups):
        own_kv(g, 0).wait()
        kv[0, g, 0] = own_keys[g].T
        own_kv(g, 1).wait()

    pl.semaphore_wait(barrier, greeted)

    def send(half, src_slot, dst_slot, g, send_sem, ctx):
        return pltpu.make_async_remote_copy(
            src_ref=kv.at[src_slot, g],
            dst_ref=kv.at[dst_slot, g],
            send_sem=send_sem.at[half, g],
            recv_sem=recv_sem.at[dst_slot, g],
            device_id={"ctx": ctx},
            device_id_type=MESH,
        )

    def arrived(d, g):
        send(0, 0, d, g, fwd_sem, me + 1 - 2 * core).wait_recv()

    def forward(n, act):
        half, g = n // groups, lax.rem(n, groups)
        e = 2 * half
        held = jnp.minimum(jnp.maximum(me - e + 1, 0), 1) * has_next

        @pl.when(held * jnp.minimum(jnp.maximum(back - e - 1, 0), 1) == 1)
        def _():
            act(send(half, e, e + 2, g, fwd_sem, me + 2))

        if back % 2 == 1:
            @pl.when((held * core == 1) & (e + 1 == back))
            def _():
                act(send(half, e, e + 1, g, fwd_sem, me + 1))

    def relay(e, g, act):
        copy = send(e // 2, e, e + 1 - 2 * core, g, relay_sem, me + 1 - 2 * core)
        if e == 0:
            pl.when(core == 0)(lambda: act(copy))
        elif e + 1 <= back:
            act(copy)
        else:
            pl.when(core == 1)(lambda: act(copy))

    def start(copy):
        copy.start()

    def finish(copy):
        copy.wait_send()

    for n in range(ahead):
        forward(jnp.int32(n), start)

    def pass_on(g, carry):
        relay(0, g, start)
        return carry

    lax.fori_loop(0, groups, pass_on, 0)

    squares[...] = jnp.zeros_like(squares)
    own_gain.wait()
    wide_gain_v[...] = gain_v[...].astype(jnp.float32)
    give_gain.start()

    def attend(j, g):
        slots = steps[j]
        k = jnp.concatenate([kv[d, g, 0] for d in slots], axis=1)
        v = jnp.concatenate([kv[d, g, 1] for d in slots], axis=0)
        v = jnp.concatenate([v, jnp.ones_like(v)], axis=1)
        limit = jnp.concatenate([cap[d] for d in slots], axis=1)
        first_head = g * ratio

        def scores(u):
            q = jnp.concatenate(
                [q_v[g, :, h * HEAD_SIZE:(h + 1) * HEAD_SIZE] for h in range(u, u + UNIT)], axis=0
            )
            return jnp.dot(q, k, preferred_element_type=jnp.float32)

        square = None
        following = scores(0)
        for u in range(0, ratio, UNIT):
            s = following
            if u + UNIT < ratio:
                following = scores(u + UNIT)
            olds, held = [], []
            if j > 0:
                olds = [top[first_head + u + n] for n in range(UNIT)]
                held = [acc[first_head + u + n] for n in range(UNIT)]
            probs, tops = [], []
            for n in range(UNIT):
                part = jnp.minimum(s[n * rows:(n + 1) * rows], limit)
                high = jnp.broadcast_to(
                    jnp.max(part, axis=1, keepdims=True), (rows, HEAD_SIZE)
                )
                if j > 0:
                    high = jnp.maximum(olds[n], high)
                tops.append(high)
                wide_high = jnp.concatenate([high] * len(slots), axis=1)
                probs.append(jnp.exp2((part - wide_high) * factor).astype(jnp.bfloat16))
            update = jnp.dot(
                jnp.concatenate(probs, axis=0), v, preferred_element_type=jnp.float32
            )
            for n in range(UNIT):
                at = update[n * rows:(n + 1) * rows]
                if j > 0:
                    correct = jnp.exp2((olds[n] - tops[n]) * factor)
                    at = at + held[n] * jnp.concatenate([correct, correct], axis=1)
                h = u + n
                if j < len(steps) - 1:
                    top[first_head + h] = tops[n]
                    acc[first_head + h] = at
                else:
                    c = (at[:, :HEAD_SIZE] / at[:, HEAD_SIZE:]).astype(jnp.bfloat16)
                    out_v[g, :, h * HEAD_SIZE:(h + 1) * HEAD_SIZE] = c
                    c = c.astype(jnp.float32)
                    square = c * c if square is None else square + c * c
        if square is not None:
            squares[...] += square

    for j in range(len(steps)):
        def step(g, carry):
            if j == 0:
                own_q(g).wait()
            else:
                odd, even = 2 * j - 1, 2 * j
                if even <= back:
                    @pl.when(me >= even)
                    def _():
                        arrived(even, g)
                        relay(even, g, start)
                n = (j - 1) * groups + g

                @pl.when(n + ahead < chunks)
                def _():
                    forward(n, finish)
                    forward(n + ahead, start)

                @pl.when(me >= odd)
                def _():
                    arrived(odd, g)
            attend(j, g)
            if j == len(steps) - 1:
                write_out(g).start()
            return carry

        lax.fori_loop(0, groups, step, 0)

    mine = jnp.sum(squares[...].T, axis=0, keepdims=True)
    sums[...] = jnp.broadcast_to(mine, sums.shape)
    copies = []
    for o in range(1, tp_size):
        copies.append(pltpu.make_async_remote_copy(
            src_ref=sums,
            dst_ref=sums_in.at[o - 1],
            send_sem=tp_send.at[o - 1],
            recv_sem=tp_recv.at[o - 1],
            device_id={"tp": lax.rem(my_tp + o, tp_size)},
            device_id_type=MESH,
        ))
        copies[-1].start()

    def drain(g, carry):
        for e in range(0, back + 1, 2):
            if e == 0:
                relay(e, g, finish)
            else:
                pl.when(me >= e)(lambda: relay(e, g, finish))
        write_out(g).wait()
        return carry

    lax.fori_loop(0, groups, drain, 0)
    for n in range(chunks - ahead, chunks):
        forward(jnp.int32(n), finish)
    total = mine
    for o, copy in enumerate(copies):
        copy.wait()
        total = total + sums_in[o, 0:1, :]
    power = total / (QUERY_HEADS * HEAD_SIZE)
    inverse = 1.0 / jnp.sqrt(power + 1e-06)
    inverse_v[...] = jnp.broadcast_to(inverse, (rows, rows)).T
    give_inverse = pltpu.make_async_copy(inverse_v, inverse_ref, len_sem)
    give_inverse.start()
    give_gain.wait()
    give_inverse.wait()


def body(ctx_size, tp_size, query, keys, values, doc_lengths, gain):
    rows = query.shape[0]
    groups = keys.shape[1] // HEAD_SIZE
    heads = query.shape[1] // HEAD_SIZE
    ratio = heads // groups
    longest = rows * ctx_size * 5 // 8
    back = min(-(-(longest - 1) // rows), ctx_size - 1)
    halves = back // 2 + 1
    gain_rows = gain.shape[0] // HEAD_SIZE
    context, inverse, wide_gain = pl.pallas_call(
        functools.partial(attention_kernel, ctx_size, tp_size, back, ratio),
        out_shape=(
            pltpu.VMEM(query.shape, jnp.bfloat16),
            pltpu.VMEM((rows, rows), jnp.float32),
            pltpu.VMEM((gain_rows, HEAD_SIZE), jnp.float32),
        ),
        in_specs=[pl.BlockSpec(memory_space=pltpu.HBM)] * 5,
        out_specs=(
            pl.BlockSpec(memory_space=pl.ANY),
            pl.BlockSpec(memory_space=pl.ANY),
            pl.BlockSpec(memory_space=pl.ANY),
        ),
        scratch_shapes=[
            pltpu.VMEM((back + 1, groups, 2, rows, HEAD_SIZE), jnp.bfloat16),
            pltpu.VMEM((groups, rows, HEAD_SIZE), jnp.bfloat16),
            pltpu.VMEM((groups, rows, ratio * HEAD_SIZE), jnp.bfloat16),
            pltpu.VMEM((groups, rows, ratio * HEAD_SIZE), jnp.bfloat16),
            pltpu.SMEM(doc_lengths.shape, jnp.int32),
            pltpu.VMEM((back + 1, rows, rows), jnp.float32),
            pltpu.VMEM((heads, rows, HEAD_SIZE), jnp.float32),
            pltpu.VMEM((heads, rows, 2 * HEAD_SIZE), jnp.float32),
            pltpu.VMEM((rows, HEAD_SIZE), jnp.float32),
            pltpu.VMEM((8, rows), jnp.float32),
            pltpu.VMEM((tp_size, 8, rows), jnp.float32),
            pltpu.VMEM((gain_rows, HEAD_SIZE), jnp.bfloat16),
            pltpu.VMEM((gain_rows, HEAD_SIZE), jnp.float32),
            pltpu.VMEM((rows, rows), jnp.float32),
            pltpu.SemaphoreType.DMA((2, groups)),
            pltpu.SemaphoreType.DMA((groups,)),
            pltpu.SemaphoreType.DMA,
            pltpu.SemaphoreType.DMA((2,)),
            pltpu.SemaphoreType.DMA((groups,)),
            pltpu.SemaphoreType.DMA((back + 1, groups)),
            pltpu.SemaphoreType.DMA((halves, groups)),
            pltpu.SemaphoreType.DMA((halves, groups)),
            pltpu.SemaphoreType.DMA((tp_size,)),
            pltpu.SemaphoreType.DMA((tp_size,)),
        ],
        compiler_params=pltpu.CompilerParams(
            collective_id=0, has_side_effects=True, vmem_limit_bytes=56 * 2**20
        ),
        cost_estimate=pl.CostEstimate(
            flops=4 * heads * rows * (back + 1) * rows * HEAD_SIZE,
            bytes_accessed=4 * query.size + 4 * keys.size,
            transcendentals=heads * rows * (back + 1) * rows,
        ),
    )(query, keys, values, doc_lengths, gain.reshape(gain_rows, HEAD_SIZE))
    return (
        context.astype(jnp.float32) * wide_gain.reshape(1, -1) * inverse[:, :1]
    ).astype(jnp.bfloat16)


def solution(mesh):
    return jax.shard_map(
        functools.partial(body, mesh.shape["ctx"], mesh.shape["tp"]),
        mesh=mesh,
        in_specs=(
            P(("dp", "ctx"), "tp"),
            P(("dp", "ctx"), "tp"),
            P(("dp", "ctx"), "tp"),
            P("dp"),
            P("tp"),
        ),
        out_specs=P(("dp", "ctx"), "tp"),
        check_vma=False,
    )
```

```python
import functools
import math

import jax
import jax.numpy as jnp
from jax import lax
from jax.experimental import pallas as pl
from jax.experimental.pallas import tpu as pltpu
from jax.sharding import PartitionSpec as P

QUERY_HEADS = 96
HEAD_SIZE = 128
LOW = -1e31
MESH = pl.DeviceIdType.MESH
UNIT = 4
STEP = 5
AHEAD = 3


def attention_kernel(
    ctx_size, tp_size, back, ratio,
    query_ref, keys_ref, values_ref, lengths_ref, gain_ref,
    context_ref, inverse_ref, wide_gain_ref,
    kv, own_keys, q_v, out_v, lengths, cap, top, acc, squares, sums, sums_in, gain_v, wide_gain_v, inverse_v,
    kv_sem, q_sem, len_sem, gain_sem, out_sem,
    recv_sem, fwd_sem, relay_sem, tp_send, tp_recv,
):
    rows = query_ref.shape[0]
    groups = keys_ref.shape[1] // HEAD_SIZE
    wide = ratio * HEAD_SIZE
    steps = [list(range(d, min(d + STEP, back + 1))) for d in range(0, back + 1, STEP)]
    phases = (back + 1) // 2
    chunks = phases * groups
    ahead = min(AHEAD, groups)
    docs = lengths.shape[0]
    chips = ctx_size // 2
    me = lax.axis_index("ctx")
    my_tp = lax.axis_index("tp")
    chip = me // 2
    core = me % 2
    has_next = (chip + 1 < chips).astype(jnp.int32)
    factor = HEAD_SIZE ** (-0.5) * math.log2(math.e)

    def columns(g, width):
        return pl.ds(pl.multiple_of(g * width, width), width)

    def own_kv(g, which):
        src = (keys_ref, values_ref)[which]
        dst = (own_keys.at[g], kv.at[0, g, 1])[which]
        return pltpu.make_async_copy(src.at[:, columns(g, HEAD_SIZE)], dst, kv_sem.at[which, g])

    def own_q(g):
        return pltpu.make_async_copy(query_ref.at[:, columns(g, wide)], q_v.at[g], q_sem.at[g])

    def write_out(g):
        return pltpu.make_async_copy(out_v.at[g], context_ref.at[:, columns(g, wide)], out_sem.at[g])

    own_lengths = pltpu.make_async_copy(lengths_ref, lengths, len_sem)
    own_gain = pltpu.make_async_copy(gain_ref, gain_v, gain_sem.at[0])
    give_gain = pltpu.make_async_copy(wide_gain_v, wide_gain_ref, gain_sem.at[1])

    for g in range(groups):
        own_kv(g, 0).start()
        own_kv(g, 1).start()
    own_lengths.start()
    for g in range(groups):
        own_q(g).start()
    own_gain.start()

    barrier = pltpu.get_barrier_semaphore()

    def greet(ctx):
        pl.semaphore_signal(barrier, inc=1, device_id={"ctx": ctx}, device_id_type=MESH)

    greet(me + 1 - 2 * core)

    @pl.when(has_next == 1)
    def _():
        greet(me + 2)

    @pl.when(chip > 0)
    def _():
        greet(me - 2)

    @pl.when(core * has_next == 1)
    def _():
        greet(me + 1)

    @pl.when((1 - core) * chip > 0)
    def _():
        greet(me - 1)

    for o in range(1, tp_size):
        pl.semaphore_signal(
            barrier, inc=1, device_id={"tp": lax.rem(my_tp + o, tp_size)}, device_id_type=MESH
        )

    for d in range(1, back + 1):
        def clear():
            kv[d] = jnp.zeros_like(kv[d])
        pl.when(me < d)(clear)

    own_lengths.wait()
    position = me * rows + lax.broadcasted_iota(jnp.int32, (rows, rows), 0)
    offset = lax.broadcasted_iota(jnp.int32, (rows, rows), 1)
    first = jnp.zeros((rows, rows), jnp.int32)
    end = jnp.int32(0)
    for i in range(docs):
        end = end + lengths[i]
        first = jnp.where(position >= end, end, first)
    for d in range(back + 1):
        key = (me - d) * rows + offset
        allowed = (key >= first) & (key <= position)
        cap[d] = jnp.where(
            allowed, jnp.float32(jnp.inf), jnp.float32(LOW)
        )

    has_last = jnp.minimum(chip, 1)
    greeted = tp_size + has_next + has_last + core * has_next + (1 - core) * has_last

    for g in range(groups):
        own_kv(g, 0).wait()
        kv[0, g, 0] = own_keys[g].T
        own_kv(g, 1).wait()

    pl.semaphore_wait(barrier, greeted)

    def send(half, src_slot, dst_slot, g, send_sem, ctx):
        return pltpu.make_async_remote_copy(
            src_ref=kv.at[src_slot, g],
            dst_ref=kv.at[dst_slot, g],
            send_sem=send_sem.at[half, g],
            recv_sem=recv_sem.at[dst_slot, g],
            device_id={"ctx": ctx},
            device_id_type=MESH,
        )

    def arrived(d, g):
        send(0, 0, d, g, fwd_sem, me + 1 - 2 * core).wait_recv()

    def forward(n, act):
        half, g = n // groups, lax.rem(n, groups)
        e = 2 * half
        held = jnp.minimum(jnp.maximum(me - e + 1, 0), 1) * has_next

        @pl.when(held * jnp.minimum(jnp.maximum(back - e - 1, 0), 1) == 1)
        def _():
            act(send(half, e, e + 2, g, fwd_sem, me + 2))

        if back % 2 == 1:
            @pl.when((held * core == 1) & (e + 1 == back))
            def _():
                act(send(half, e, e + 1, g, fwd_sem, me + 1))

    def relay(e, g, act):
        copy = send(e // 2, e, e + 1 - 2 * core, g, relay_sem, me + 1 - 2 * core)
        if e == 0:
            pl.when(core == 0)(lambda: act(copy))
        elif e + 1 <= back:
            act(copy)
        else:
            pl.when(core == 1)(lambda: act(copy))

    def start(copy):
        copy.start()

    def finish(copy):
        copy.wait_send()

    for n in range(ahead):
        forward(jnp.int32(n), start)

    def pass_on(g, carry):
        relay(0, g, start)
        return carry

    lax.fori_loop(0, groups, pass_on, 0)

    squares[...] = jnp.zeros_like(squares)
    own_gain.wait()
    wide_gain_v[...] = gain_v[...].astype(jnp.float32)
    give_gain.start()

    def attend(j, g):
        slots = steps[j]
        k = jnp.concatenate([kv[d, g, 0] for d in slots], axis=1)
        v = jnp.concatenate([kv[d, g, 1] for d in slots], axis=0)
        v = jnp.concatenate([v, jnp.ones_like(v)], axis=1)
        limit = jnp.concatenate([cap[d] for d in slots], axis=1)
        first_head = g * ratio

        def scores(u):
            q = jnp.concatenate(
                [q_v[g, :, h * HEAD_SIZE:(h + 1) * HEAD_SIZE] for h in range(u, u + UNIT)], axis=0
            )
            return jnp.dot(q, k, preferred_element_type=jnp.float32)

        square = None
        following = scores(0)
        for u in range(0, ratio, UNIT):
            s = following
            if u + UNIT < ratio:
                following = scores(u + UNIT)
            olds, held = [], []
            if j > 0:
                olds = [top[first_head + u + n] for n in range(UNIT)]
                held = [acc[first_head + u + n] for n in range(UNIT)]
            probs, tops = [], []
            for n in range(UNIT):
                part = jnp.minimum(s[n * rows:(n + 1) * rows], limit)
                high = jnp.broadcast_to(
                    jnp.max(part, axis=1, keepdims=True), (rows, HEAD_SIZE)
                )
                if j > 0:
                    high = jnp.maximum(olds[n], high)
                tops.append(high)
                wide_high = jnp.concatenate([high] * len(slots), axis=1)
                probs.append(jnp.exp2((part - wide_high) * factor).astype(jnp.bfloat16))
            update = jnp.dot(
                jnp.concatenate(probs, axis=0), v, preferred_element_type=jnp.float32
            )
            for n in range(UNIT):
                at = update[n * rows:(n + 1) * rows]
                if j > 0:
                    correct = jnp.exp2((olds[n] - tops[n]) * factor)
                    at = at + held[n] * jnp.concatenate([correct, correct], axis=1)
                h = u + n
                if j < len(steps) - 1:
                    top[first_head + h] = tops[n]
                    acc[first_head + h] = at
                else:
                    c = (at[:, :HEAD_SIZE] / at[:, HEAD_SIZE:]).astype(jnp.bfloat16)
                    out_v[g, :, h * HEAD_SIZE:(h + 1) * HEAD_SIZE] = c
                    c = c.astype(jnp.float32)
                    square = c * c if square is None else square + c * c
        if square is not None:
            squares[...] += square

    for p in range(phases):
        def phase(g, carry):
            even = 2 * p + 2
            if even <= back:
                @pl.when(me >= even)
                def _():
                    arrived(even, g)
                    relay(even, g, start)
            n = p * groups + g

            @pl.when(n + ahead < chunks)
            def _():
                forward(n, finish)
                forward(n + ahead, start)

            for j, slots in enumerate(steps):
                if (slots[-1] + 1) // 2 - 1 != p:
                    continue
                for d in slots:
                    if d % 2 == 1:
                        pl.when(me >= d)(lambda d=d: arrived(d, g))
                if j == 0:
                    own_q(g).wait()
                attend(j, g)
                if j == len(steps) - 1:
                    write_out(g).start()
            return carry

        lax.fori_loop(0, groups, phase, 0)

    mine = jnp.sum(squares[...].T, axis=0, keepdims=True)
    sums[...] = jnp.broadcast_to(mine, sums.shape)
    copies = []
    for o in range(1, tp_size):
        copies.append(pltpu.make_async_remote_copy(
            src_ref=sums,
            dst_ref=sums_in.at[o - 1],
            send_sem=tp_send.at[o - 1],
            recv_sem=tp_recv.at[o - 1],
            device_id={"tp": lax.rem(my_tp + o, tp_size)},
            device_id_type=MESH,
        ))
        copies[-1].start()

    def drain(g, carry):
        for e in range(0, back + 1, 2):
            if e == 0:
                relay(e, g, finish)
            else:
                pl.when(me >= e)(lambda: relay(e, g, finish))
        write_out(g).wait()
        return carry

    lax.fori_loop(0, groups, drain, 0)
    for n in range(chunks - ahead, chunks):
        forward(jnp.int32(n), finish)
    total = mine
    for o, copy in enumerate(copies):
        copy.wait()
        total = total + sums_in[o, 0:1, :]
    power = total / (QUERY_HEADS * HEAD_SIZE)
    inverse = 1.0 / jnp.sqrt(power + 1e-06)
    inverse_v[...] = jnp.broadcast_to(inverse, (rows, rows)).T
    give_inverse = pltpu.make_async_copy(inverse_v, inverse_ref, len_sem)
    give_inverse.start()
    give_gain.wait()
    give_inverse.wait()


def body(ctx_size, tp_size, query, keys, values, doc_lengths, gain):
    rows = query.shape[0]
    groups = keys.shape[1] // HEAD_SIZE
    heads = query.shape[1] // HEAD_SIZE
    ratio = heads // groups
    longest = rows * ctx_size * 5 // 8
    back = min(-(-(longest - 1) // rows), ctx_size - 1)
    halves = back // 2 + 1
    gain_rows = gain.shape[0] // HEAD_SIZE
    context, inverse, wide_gain = pl.pallas_call(
        functools.partial(attention_kernel, ctx_size, tp_size, back, ratio),
        out_shape=(
            pltpu.VMEM(query.shape, jnp.bfloat16),
            pltpu.VMEM((rows, rows), jnp.float32),
            pltpu.VMEM((gain_rows, HEAD_SIZE), jnp.float32),
        ),
        in_specs=[pl.BlockSpec(memory_space=pltpu.HBM)] * 5,
        out_specs=(
            pl.BlockSpec(memory_space=pl.ANY),
            pl.BlockSpec(memory_space=pl.ANY),
            pl.BlockSpec(memory_space=pl.ANY),
        ),
        scratch_shapes=[
            pltpu.VMEM((back + 1, groups, 2, rows, HEAD_SIZE), jnp.bfloat16),
            pltpu.VMEM((groups, rows, HEAD_SIZE), jnp.bfloat16),
            pltpu.VMEM((groups, rows, ratio * HEAD_SIZE), jnp.bfloat16),
            pltpu.VMEM((groups, rows, ratio * HEAD_SIZE), jnp.bfloat16),
            pltpu.SMEM(doc_lengths.shape, jnp.int32),
            pltpu.VMEM((back + 1, rows, rows), jnp.float32),
            pltpu.VMEM((heads, rows, HEAD_SIZE), jnp.float32),
            pltpu.VMEM((heads, rows, 2 * HEAD_SIZE), jnp.float32),
            pltpu.VMEM((rows, HEAD_SIZE), jnp.float32),
            pltpu.VMEM((8, rows), jnp.float32),
            pltpu.VMEM((tp_size, 8, rows), jnp.float32),
            pltpu.VMEM((gain_rows, HEAD_SIZE), jnp.bfloat16),
            pltpu.VMEM((gain_rows, HEAD_SIZE), jnp.float32),
            pltpu.VMEM((rows, rows), jnp.float32),
            pltpu.SemaphoreType.DMA((2, groups)),
            pltpu.SemaphoreType.DMA((groups,)),
            pltpu.SemaphoreType.DMA,
            pltpu.SemaphoreType.DMA((2,)),
            pltpu.SemaphoreType.DMA((groups,)),
            pltpu.SemaphoreType.DMA((back + 1, groups)),
            pltpu.SemaphoreType.DMA((halves, groups)),
            pltpu.SemaphoreType.DMA((halves, groups)),
            pltpu.SemaphoreType.DMA((tp_size,)),
            pltpu.SemaphoreType.DMA((tp_size,)),
        ],
        compiler_params=pltpu.CompilerParams(
            collective_id=0, has_side_effects=True, vmem_limit_bytes=56 * 2**20
        ),
        cost_estimate=pl.CostEstimate(
            flops=4 * heads * rows * (back + 1) * rows * HEAD_SIZE,
            bytes_accessed=4 * query.size + 4 * keys.size,
            transcendentals=heads * rows * (back + 1) * rows,
        ),
    )(query, keys, values, doc_lengths, gain.reshape(gain_rows, HEAD_SIZE))
    return (
        context.astype(jnp.float32) * wide_gain.reshape(1, -1) * inverse[:, :1]
    ).astype(jnp.bfloat16)


def solution(mesh):
    return jax.shard_map(
        functools.partial(body, mesh.shape["ctx"], mesh.shape["tp"]),
        mesh=mesh,
        in_specs=(
            P(("dp", "ctx"), "tp"),
            P(("dp", "ctx"), "tp"),
            P(("dp", "ctx"), "tp"),
            P("dp"),
            P("tp"),
        ),
        out_specs=P(("dp", "ctx"), "tp"),
        check_vma=False,
    )
```

```python
import functools
import math

import jax
import jax.numpy as jnp
from jax import lax
from jax.experimental import pallas as pl
from jax.experimental.pallas import tpu as pltpu
from jax.sharding import PartitionSpec as P

QUERY_HEADS = 96
HEAD_SIZE = 128
LOW = -1e31
MESH = pl.DeviceIdType.MESH
UNIT = 4
STEP = 2
AHEAD = 3


def attention_kernel(
    ctx_size, tp_size, back, ratio,
    query_ref, keys_ref, values_ref, lengths_ref, gain_ref,
    context_ref, inverse_ref, wide_gain_ref,
    kv, own_keys, q_v, out_v, lengths, cap, top, acc, squares, sums, sums_in, gain_v, wide_gain_v, inverse_v,
    kv_sem, q_sem, len_sem, gain_sem, out_sem,
    recv_sem, fwd_sem, relay_sem, tp_send, tp_recv,
):
    rows = query_ref.shape[0]
    groups = keys_ref.shape[1] // HEAD_SIZE
    wide = ratio * HEAD_SIZE
    steps = [list(range(d, min(d + STEP, back + 1))) for d in range(0, back + 1, STEP)]
    phases = (back + 1) // 2
    chunks = phases * groups
    ahead = min(AHEAD, groups)
    docs = lengths.shape[0]
    chips = ctx_size // 2
    me = lax.axis_index("ctx")
    my_tp = lax.axis_index("tp")
    chip = me // 2
    core = me % 2
    has_next = (chip + 1 < chips).astype(jnp.int32)
    factor = HEAD_SIZE ** (-0.5) * math.log2(math.e)

    def columns(g, width):
        return pl.ds(pl.multiple_of(g * width, width), width)

    def own_kv(g, which):
        src = (keys_ref, values_ref)[which]
        dst = (own_keys.at[g], kv.at[0, g, 1])[which]
        return pltpu.make_async_copy(src.at[:, columns(g, HEAD_SIZE)], dst, kv_sem.at[which, g])

    def own_q(g):
        return pltpu.make_async_copy(query_ref.at[:, columns(g, wide)], q_v.at[g], q_sem.at[g])

    def write_out(g):
        return pltpu.make_async_copy(out_v.at[g], context_ref.at[:, columns(g, wide)], out_sem.at[g])

    own_lengths = pltpu.make_async_copy(lengths_ref, lengths, len_sem)
    own_gain = pltpu.make_async_copy(gain_ref, gain_v, gain_sem.at[0])
    give_gain = pltpu.make_async_copy(wide_gain_v, wide_gain_ref, gain_sem.at[1])

    for g in range(groups):
        own_kv(g, 0).start()
        own_kv(g, 1).start()
    own_lengths.start()
    for g in range(groups):
        own_q(g).start()
    own_gain.start()

    barrier = pltpu.get_barrier_semaphore()

    def greet(ctx):
        pl.semaphore_signal(barrier, inc=1, device_id={"ctx": ctx}, device_id_type=MESH)

    greet(me + 1 - 2 * core)

    @pl.when(has_next == 1)
    def _():
        greet(me + 2)

    @pl.when(chip > 0)
    def _():
        greet(me - 2)

    @pl.when(core * has_next == 1)
    def _():
        greet(me + 1)

    @pl.when((1 - core) * chip > 0)
    def _():
        greet(me - 1)

    for o in range(1, tp_size):
        pl.semaphore_signal(
            barrier, inc=1, device_id={"tp": lax.rem(my_tp + o, tp_size)}, device_id_type=MESH
        )

    for d in range(1, back + 1):
        def clear():
            kv[d] = jnp.zeros_like(kv[d])
        pl.when(me < d)(clear)

    own_lengths.wait()
    position = me * rows + lax.broadcasted_iota(jnp.int32, (rows, rows), 0)
    offset = lax.broadcasted_iota(jnp.int32, (rows, rows), 1)
    first = jnp.zeros((rows, rows), jnp.int32)
    end = jnp.int32(0)
    for i in range(docs):
        end = end + lengths[i]
        first = jnp.where(position >= end, end, first)
    for d in range(back + 1):
        key = (me - d) * rows + offset
        allowed = (key >= first) & (key <= position)
        cap[d] = jnp.where(
            allowed, jnp.float32(jnp.inf), jnp.float32(LOW)
        )

    has_last = jnp.minimum(chip, 1)
    greeted = tp_size + has_next + has_last + core * has_next + (1 - core) * has_last

    for g in range(groups):
        own_kv(g, 0).wait()
        kv[0, g, 0] = own_keys[g].T
        own_kv(g, 1).wait()

    pl.semaphore_wait(barrier, greeted)

    def send(half, src_slot, dst_slot, g, send_sem, ctx):
        return pltpu.make_async_remote_copy(
            src_ref=kv.at[src_slot, g],
            dst_ref=kv.at[dst_slot, g],
            send_sem=send_sem.at[half, g],
            recv_sem=recv_sem.at[dst_slot, g],
            device_id={"ctx": ctx},
            device_id_type=MESH,
        )

    def arrived(d, g):
        send(0, 0, d, g, fwd_sem, me + 1 - 2 * core).wait_recv()

    def forward(n, act):
        half, g = n // groups, lax.rem(n, groups)
        e = 2 * half
        held = jnp.minimum(jnp.maximum(me - e + 1, 0), 1) * has_next

        @pl.when(held * jnp.minimum(jnp.maximum(back - e - 1, 0), 1) == 1)
        def _():
            act(send(half, e, e + 2, g, fwd_sem, me + 2))

        if back % 2 == 1:
            @pl.when((held * core == 1) & (e + 1 == back))
            def _():
                act(send(half, e, e + 1, g, fwd_sem, me + 1))

    def relay(e, g, act):
        copy = send(e // 2, e, e + 1 - 2 * core, g, relay_sem, me + 1 - 2 * core)
        if e == 0:
            pl.when(core == 0)(lambda: act(copy))
        elif e + 1 <= back:
            act(copy)
        else:
            pl.when(core == 1)(lambda: act(copy))

    def start(copy):
        copy.start()

    def finish(copy):
        copy.wait_send()

    for n in range(ahead):
        forward(jnp.int32(n), start)

    def pass_on(g, carry):
        relay(0, g, start)
        return carry

    lax.fori_loop(0, groups, pass_on, 0)

    squares[...] = jnp.zeros_like(squares)
    own_gain.wait()
    wide_gain_v[...] = gain_v[...].astype(jnp.float32)
    give_gain.start()

    def attend(j, g):
        slots = steps[j]
        k = jnp.concatenate([kv[d, g, 0] for d in slots], axis=1)
        v = jnp.concatenate([kv[d, g, 1] for d in slots], axis=0)
        v = jnp.concatenate([v, jnp.ones_like(v)], axis=1)
        limit = jnp.concatenate([cap[d] for d in slots], axis=1)
        first_head = g * ratio

        def scores(u):
            q = jnp.concatenate(
                [q_v[g, :, h * HEAD_SIZE:(h + 1) * HEAD_SIZE] for h in range(u, u + UNIT)], axis=0
            )
            return jnp.dot(q, k, preferred_element_type=jnp.float32)

        square = None
        following = scores(0)
        for u in range(0, ratio, UNIT):
            s = following
            if u + UNIT < ratio:
                following = scores(u + UNIT)
            olds, held = [], []
            if j > 0:
                olds = [top[first_head + u + n] for n in range(UNIT)]
                held = [acc[first_head + u + n] for n in range(UNIT)]
            probs, tops = [], []
            for n in range(UNIT):
                part = jnp.minimum(s[n * rows:(n + 1) * rows], limit)
                high = jnp.broadcast_to(
                    jnp.max(part, axis=1, keepdims=True), (rows, HEAD_SIZE)
                )
                if j > 0:
                    high = jnp.maximum(olds[n], high)
                tops.append(high)
                wide_high = jnp.concatenate([high] * len(slots), axis=1)
                probs.append(jnp.exp2((part - wide_high) * factor).astype(jnp.bfloat16))
            update = jnp.dot(
                jnp.concatenate(probs, axis=0), v, preferred_element_type=jnp.float32
            )
            for n in range(UNIT):
                at = update[n * rows:(n + 1) * rows]
                if j > 0:
                    correct = jnp.exp2((olds[n] - tops[n]) * factor)
                    at = at + held[n] * jnp.concatenate([correct, correct], axis=1)
                h = u + n
                if j < len(steps) - 1:
                    top[first_head + h] = tops[n]
                    acc[first_head + h] = at
                else:
                    c = (at[:, :HEAD_SIZE] / at[:, HEAD_SIZE:]).astype(jnp.bfloat16)
                    out_v[g, :, h * HEAD_SIZE:(h + 1) * HEAD_SIZE] = c
                    c = c.astype(jnp.float32)
                    square = c * c if square is None else square + c * c
        if square is not None:
            squares[...] += square

    for p in range(phases):
        def phase(g, carry):
            even = 2 * p + 2
            if even <= back:
                @pl.when(me >= even)
                def _():
                    arrived(even, g)
                    relay(even, g, start)
            n = p * groups + g

            @pl.when(n + ahead < chunks)
            def _():
                forward(n, finish)
                forward(n + ahead, start)

            for j, slots in enumerate(steps):
                if (slots[-1] + 1) // 2 - 1 != p:
                    continue
                for d in slots:
                    if d % 2 == 1:
                        pl.when(me >= d)(lambda d=d: arrived(d, g))
                if j == 0:
                    own_q(g).wait()
                attend(j, g)
                if j == len(steps) - 1:
                    write_out(g).start()
            return carry

        lax.fori_loop(0, groups, phase, 0)

    mine = jnp.sum(squares[...].T, axis=0, keepdims=True)
    sums[...] = jnp.broadcast_to(mine, sums.shape)
    copies = []
    for o in range(1, tp_size):
        copies.append(pltpu.make_async_remote_copy(
            src_ref=sums,
            dst_ref=sums_in.at[o - 1],
            send_sem=tp_send.at[o - 1],
            recv_sem=tp_recv.at[o - 1],
            device_id={"tp": lax.rem(my_tp + o, tp_size)},
            device_id_type=MESH,
        ))
        copies[-1].start()

    def drain(g, carry):
        for e in range(0, back + 1, 2):
            if e == 0:
                relay(e, g, finish)
            else:
                pl.when(me >= e)(lambda: relay(e, g, finish))
        write_out(g).wait()
        return carry

    lax.fori_loop(0, groups, drain, 0)
    for n in range(chunks - ahead, chunks):
        forward(jnp.int32(n), finish)
    total = mine
    for o, copy in enumerate(copies):
        copy.wait()
        total = total + sums_in[o, 0:1, :]
    power = total / (QUERY_HEADS * HEAD_SIZE)
    inverse = 1.0 / jnp.sqrt(power + 1e-06)
    inverse_v[...] = jnp.broadcast_to(inverse, (rows, rows)).T
    give_inverse = pltpu.make_async_copy(inverse_v, inverse_ref, len_sem)
    give_inverse.start()
    give_gain.wait()
    give_inverse.wait()


def body(ctx_size, tp_size, query, keys, values, doc_lengths, gain):
    rows = query.shape[0]
    groups = keys.shape[1] // HEAD_SIZE
    heads = query.shape[1] // HEAD_SIZE
    ratio = heads // groups
    longest = rows * ctx_size * 5 // 8
    back = min(-(-(longest - 1) // rows), ctx_size - 1)
    halves = back // 2 + 1
    gain_rows = gain.shape[0] // HEAD_SIZE
    context, inverse, wide_gain = pl.pallas_call(
        functools.partial(attention_kernel, ctx_size, tp_size, back, ratio),
        out_shape=(
            pltpu.VMEM(query.shape, jnp.bfloat16),
            pltpu.VMEM((rows, rows), jnp.float32),
            pltpu.VMEM((gain_rows, HEAD_SIZE), jnp.float32),
        ),
        in_specs=[pl.BlockSpec(memory_space=pltpu.HBM)] * 5,
        out_specs=(
            pl.BlockSpec(memory_space=pl.ANY),
            pl.BlockSpec(memory_space=pl.ANY),
            pl.BlockSpec(memory_space=pl.ANY),
        ),
        scratch_shapes=[
            pltpu.VMEM((back + 1, groups, 2, rows, HEAD_SIZE), jnp.bfloat16),
            pltpu.VMEM((groups, rows, HEAD_SIZE), jnp.bfloat16),
            pltpu.VMEM((groups, rows, ratio * HEAD_SIZE), jnp.bfloat16),
            pltpu.VMEM((groups, rows, ratio * HEAD_SIZE), jnp.bfloat16),
            pltpu.SMEM(doc_lengths.shape, jnp.int32),
            pltpu.VMEM((back + 1, rows, rows), jnp.float32),
            pltpu.VMEM((heads, rows, HEAD_SIZE), jnp.float32),
            pltpu.VMEM((heads, rows, 2 * HEAD_SIZE), jnp.float32),
            pltpu.VMEM((rows, HEAD_SIZE), jnp.float32),
            pltpu.VMEM((8, rows), jnp.float32),
            pltpu.VMEM((tp_size, 8, rows), jnp.float32),
            pltpu.VMEM((gain_rows, HEAD_SIZE), jnp.bfloat16),
            pltpu.VMEM((gain_rows, HEAD_SIZE), jnp.float32),
            pltpu.VMEM((rows, rows), jnp.float32),
            pltpu.SemaphoreType.DMA((2, groups)),
            pltpu.SemaphoreType.DMA((groups,)),
            pltpu.SemaphoreType.DMA,
            pltpu.SemaphoreType.DMA((2,)),
            pltpu.SemaphoreType.DMA((groups,)),
            pltpu.SemaphoreType.DMA((back + 1, groups)),
            pltpu.SemaphoreType.DMA((halves, groups)),
            pltpu.SemaphoreType.DMA((halves, groups)),
            pltpu.SemaphoreType.DMA((tp_size,)),
            pltpu.SemaphoreType.DMA((tp_size,)),
        ],
        compiler_params=pltpu.CompilerParams(
            collective_id=0, has_side_effects=True, vmem_limit_bytes=56 * 2**20
        ),
        cost_estimate=pl.CostEstimate(
            flops=4 * heads * rows * (back + 1) * rows * HEAD_SIZE,
            bytes_accessed=4 * query.size + 4 * keys.size,
            transcendentals=heads * rows * (back + 1) * rows,
        ),
    )(query, keys, values, doc_lengths, gain.reshape(gain_rows, HEAD_SIZE))
    return (
        context.astype(jnp.float32) * wide_gain.reshape(1, -1) * inverse[:, :1]
    ).astype(jnp.bfloat16)


def solution(mesh):
    return jax.shard_map(
        functools.partial(body, mesh.shape["ctx"], mesh.shape["tp"]),
        mesh=mesh,
        in_specs=(
            P(("dp", "ctx"), "tp"),
            P(("dp", "ctx"), "tp"),
            P(("dp", "ctx"), "tp"),
            P("dp"),
            P("tp"),
        ),
        out_specs=P(("dp", "ctx"), "tp"),
        check_vma=False,
    )
```
